256 devices in a mesh: rad: 8 (over z), mode: 32 (over x, y, core).
Axes of the slice: x: 4, y: 4, z: 8, core: 2. Of those that a mesh axis runs over, the one named last changes fastest.
Arguments:
- forcing: bfloat16 [2, 1024, 128, 1536], P(None, 'rad', 'mode'), may hold values from -6 to 6
- spectral_state: float32 [2, 512, 8, 2, 1024], P(None, 'mode', 'rad'), may hold values from -6 to 6
- block_inverses: bfloat16 [2, 512, 8, 8, 128, 128], P(None, 'mode', 'rad'), may hold values from -0.6 to 1.2
- second_weights: float32 [9, 1024], replicated, may hold values from -1.5 to 1.5
- first_weights: float32 [9, 1024], replicated, may hold values from -1.5 to 1.5
- radial_points: float32 [1024], replicated, may hold values from 0.5 to 1, as said below
Outputs:
- solution: float32 [2, 512, 8, 2, 1024], P(None, 'mode', 'rad')
The draws below stay inside these ranges and needn't reach their ends.
Inputs may be any that keep to these rules, and one draw needn't show every extreme that they name: `radial_points`: increasing along the radius.
All inputs are finite; a program needn't handle non-finite values.
Results may differ from the reference program's by a relative error of at most 0.0021.
Values may be sent and summed in bfloat16 or wider, within the bound.
A program may use at most 64 MiB of HBM per device.

```python
import math
import jax
import jax.numpy as jnp
import numpy as np
from jax import lax

P_SIZE = 2
NR = 1024
NTH = 1536
MTH = 512
NZ = 128
KZ = 8
BK = 128
NB = 8


def draw_block_inverses(key, part):
    key = jax.random.fold_in(key, 11)
    key_off, key_diag = jax.random.split(key)
    array_shape = (P_SIZE, MTH, KZ, NB, BK, BK)
    spread = 0.6 / math.sqrt(BK)
    off_diagonal = jax.random.uniform(key_off, array_shape, dtype=jnp.float32, minval=-spread, maxval=spread)
    diagonal_part = jax.random.uniform(key_diag, (P_SIZE, MTH, KZ, NB, BK), dtype=jnp.float32, minval=0.6, maxval=1.19)
    identity = jnp.eye(BK, dtype=jnp.float32)
    return (off_diagonal * (1.0 - identity) + identity * diagonal_part[..., None]).astype(jnp.bfloat16)


def draw_radial_points(key, part):
    key = jax.random.fold_in(key, 5)
    jitter = jax.random.uniform(key, (NR,), dtype=jnp.float32)
    position = (jnp.arange(NR, dtype=jnp.float32) + jitter) / NR
    return 0.5 + 0.5 * jnp.sin(0.5 * math.pi * position)


def block_levels(rng, extent, shards, low, top_value):
    def one(axis_at, shards_of):
        steps = jax.random.uniform(jax.random.fold_in(jax.random.fold_in(rng, 6), axis_at), (shards_of,), jnp.float32, low / len(shards), top_value / len(shards))
        return jnp.repeat(jnp.exp(steps), extent[axis_at] // shards_of).reshape((-1,) + (1,) * (len(extent) - axis_at - 1))

    gain = one(*shards[0])
    for cut in shards[1:]:
        gain = gain * one(*cut)
    return gain


def gaussian(stream_key, dims, width, reach, cuts=(), kind=jnp.bfloat16):
    values = jax.random.normal(stream_key, dims, jnp.float32) * width
    if len(cuts) > 0:
        values = block_levels(stream_key, dims, cuts, -0.22, 0.18) * values
    return jnp.clip(values, min=-reach, max=reach).astype(kind)


def setup_inputs(seed: int = 0) -> dict:
    key_list = jax.random.split(jax.random.key(seed), 7)
    return {
        "forcing": gaussian(key_list[0], (P_SIZE, NR, NZ, NTH), 1.0, 6.0, ((1, 8), (2, 32))),
        "spectral_state": gaussian(key_list[1], (P_SIZE, MTH, KZ, 2, NR), 1.0, 6.0, ((1, 32), (2, 8)), jnp.float32),
        "block_inverses": draw_block_inverses(jax.random.fold_in(key_list[6], 71), 0),
        "second_weights": gaussian(key_list[3], (9, NR), 0.3, 1.5, (), jnp.float32),
        "first_weights": gaussian(key_list[4], (9, NR), 0.3, 1.5, (), jnp.float32),
        "radial_points": draw_radial_points(jax.random.fold_in(key_list[6], 71), 0),
    }


AXIAL_FACTOR = 0.05
HIGHEST = lax.Precision.HIGHEST

def azimuth_table(theta_points, mode_total):
    angle_index = jnp.arange(theta_points, dtype=jnp.int32)[:, None]
    harmonic = jnp.arange(mode_total, dtype=jnp.int32)[None, :]
    residue = angle_index * harmonic % theta_points
    radians = 2.0 * math.pi / theta_points * residue.astype(jnp.float32)
    norm_factor = 1.0 / math.sqrt(theta_points)
    result_table = jnp.stack([jnp.cos(radians) * norm_factor, -jnp.sin(radians) * norm_factor], axis=1)
    return result_table.astype(jnp.bfloat16)

def axial_table(axial_points, wave_total):
    plane_index = jnp.arange(axial_points, dtype=jnp.int32)[:, None]
    wavenumber = jnp.arange(wave_total, dtype=jnp.int32)[None, :] - wave_total // 2
    residue = wavenumber % axial_points * plane_index % axial_points
    radians = 2.0 * math.pi / axial_points * residue.astype(jnp.float32)
    norm_factor = 1.0 / math.sqrt(axial_points)
    cosine_part = jnp.cos(radians) * norm_factor
    sine_part = jnp.sin(radians) * norm_factor
    real_rows = jnp.stack([cosine_part, -sine_part], axis=-1)
    imag_rows = jnp.stack([sine_part, cosine_part], axis=-1)
    return jnp.stack([real_rows, imag_rows], axis=0).astype(jnp.bfloat16)

def explicit_terms(current_state, second_weights, first_weights, radial_points, azimuth_index, wavenumber, mode_total):
    length = current_state.shape[-1]
    padded = jnp.pad(current_state, [(0, 0)] * 4 + [(4, 4)])
    second_sum = jnp.zeros_like(current_state)
    first_sum = jnp.zeros_like(current_state)
    for offset in range(9):
        window = padded[..., offset:offset + length]
        second_sum = second_sum + second_weights[offset] * window
        first_sum = first_sum + first_weights[offset] * window
    diagonal_shift = (azimuth_index[:, None, None, None] / mode_total) ** 2 / radial_points ** 2 + AXIAL_FACTOR * wavenumber[None, :, None, None] ** 2
    return current_state + second_sum + first_sum / radial_points - diagonal_shift * current_state

def coupling(second_weights, first_weights, radial_points, first_row, reach_shift):
    row_offset = np.arange(4)[:, None]
    col_offset = np.arange(4)[None, :]
    stencil_index = reach_shift + col_offset - row_offset
    inside = (stencil_index >= 0) & (stencil_index <= 8)
    clipped = np.clip(stencil_index, 0, 8)
    row_index = first_row + row_offset + 0 * col_offset
    values = -(second_weights[clipped, row_index] + first_weights[clipped, row_index] / radial_points[row_index])
    return jnp.where(inside, values, 0.0)

def block_solve(right_side, inverses, second_weights, first_weights, radial_points):
    block_total = inverses.shape[3]
    block_size = inverses.shape[4]
    partial_list = []
    previous = None
    for block_index in range(block_total):
        portion = right_side[..., block_index * block_size:(block_index + 1) * block_size]
        if block_index > 0:
            matrix = coupling(second_weights, first_weights, radial_points, block_index * block_size, 0)
            pushed = jnp.einsum('ab,pmkcb->pmkca', matrix, previous[..., block_size - 4:], precision=HIGHEST)
            portion = jnp.concatenate([portion[..., :4] - pushed, portion[..., 4:]], axis=-1)
        current = inverses[:, :, :, block_index].astype(jnp.float32)
        previous = jnp.einsum('pmkoi,pmkci->pmkco', current, portion, precision=HIGHEST)
        partial_list.append(previous)
    following = partial_list[-1]
    outputs = [following]
    for block_index in range(block_total - 2, -1, -1):
        matrix = coupling(second_weights, first_weights, radial_points, block_index * block_size + block_size - 4, 8)
        pulled = jnp.einsum('ab,pmkcb->pmkca', matrix, following[..., :4], precision=HIGHEST)
        tail_cols = inverses[:, :, :, block_index, :, block_size - 4:].astype(jnp.float32)
        following = partial_list[block_index] - jnp.einsum('pmkoa,pmkca->pmkco', tail_cols, pulled, precision=HIGHEST)
        outputs.insert(0, following)
    return jnp.concatenate(outputs, axis=-1)

def reference(forcing, spectral_state, block_inverses, second_weights, first_weights, radial_points):
    azimuth_cols = azimuth_table(NTH, MTH)
    axial_cols = axial_table(NZ, KZ)
    spectra = jnp.einsum('przt,tcm->pmczr', forcing.astype(jnp.float32), azimuth_cols.astype(jnp.float32), precision=HIGHEST).astype(jnp.bfloat16)
    coefficients = jnp.einsum('pmczr,czkd->pmkdr', spectra.astype(jnp.float32), axial_cols.astype(jnp.float32), precision=HIGHEST)
    azimuth_index = jnp.arange(MTH, dtype=jnp.int32).astype(jnp.float32)
    wavenumber = (jnp.arange(KZ, dtype=jnp.int32) - KZ // 2).astype(jnp.float32)
    right_side = explicit_terms(spectral_state, second_weights, first_weights, radial_points, azimuth_index, wavenumber, MTH) + coefficients
    return block_solve(right_side, block_inverses, second_weights, first_weights, radial_points)
```

```python
import functools
import math

import jax
import jax.numpy as jnp
import numpy as np
from jax import lax
from jax.experimental import pallas as pl
from jax.experimental.pallas import tpu as pltpu
from jax.sharding import PartitionSpec as P

NTH = 1536
MTH = 512
NZ = 128
KZ = 8
BK = 128
NB = 8
NR = 1024
CHUNKS = 4
MC = 4


AXIAL_FACTOR = 0.05


def azimuth_table():
    t = np.arange(NTH, dtype=np.int64)[:, None]
    m = np.arange(MTH, dtype=np.int64)[None, :]
    radians = 2.0 * math.pi / NTH * ((t * m) % NTH).astype(np.float64)
    norm = 1.0 / math.sqrt(NTH)
    table = np.stack([np.cos(radians) * norm, -np.sin(radians) * norm], axis=1)
    return table.astype(np.float32).astype(jnp.bfloat16)


def axial_table():
    z = np.arange(NZ, dtype=np.int64)[:, None]
    q = np.arange(KZ, dtype=np.int64)[None, :] - KZ // 2
    radians = 2.0 * math.pi / NZ * (((q % NZ) * z) % NZ).astype(np.float64)
    norm = 1.0 / math.sqrt(NZ)
    c = np.cos(radians) * norm
    s = np.sin(radians) * norm
    table = np.stack([np.stack([c, -s], axis=-1), np.stack([s, c], axis=-1)], axis=0)
    return table.astype(np.float32).astype(jnp.bfloat16)


def border_rows(inv_ref, j, b):
    per_problem = []
    for p in range(2):
        for i in range(MC):
            top = inv_ref[p, j * MC + i, b, 0:16, :].astype(jnp.float32)
            low = inv_ref[p, j * MC + i, b, BK - 16 : BK, :].astype(jnp.float32)
            per_problem.append(jnp.concatenate([top[0:4], low[12:16]], axis=0))
    return jnp.swapaxes(jnp.stack(per_problem, axis=0), 0, 1)


def coupling_rows(weights):
    place = lax.broadcasted_iota(jnp.int32, (1, NR), 1) % BK
    below, above = [], []
    for g in range(4):
        m = jnp.zeros((1, NR), jnp.float32)
        n = jnp.zeros((1, NR), jnp.float32)
        for a in range(4):
            if g >= a:
                m = jnp.where(place == a, -weights[g - a : g - a + 1, :], m)
            if g <= a:
                n = jnp.where(place == BK - 4 + a, -weights[g - a + 8 : g - a + 9, :], n)
        below.append(m)
        above.append(n)
    return below, above


def lane_sum(value):
    return jnp.sum(value, axis=-1, keepdims=True)


def prepare(inv_ref, below_ref, above_ref, border_ref, step_ref, j, b):
    rows = border_rows(inv_ref, j, b)
    border_ref[j, b] = rows
    lanes = pl.ds(pl.multiple_of(b * BK, BK), BK)
    for g in range(4):
        m = below_ref[g : g + 1, lanes]
        n = above_ref[g : g + 1, lanes]
        for a in range(4):
            shape = (8, BK)
            step_ref[j, b, 0, a, g] = jnp.broadcast_to(lane_sum(rows[4 + a] * m), shape)
            step_ref[j, b, 1, a, g] = jnp.broadcast_to(lane_sum(rows[a] * m), shape)
            step_ref[j, b, 2, a, g] = jnp.broadcast_to(lane_sum(rows[a] * n), shape)


def solve_chunk(rhs, inv_ref, below_ref, above_ref, border_ref, step_ref, out_ref, j):
    shape = (8, BK)
    corrected = [[None] * NB for _ in range(2)]
    for d in range(2):
        tails = []
        heads = []
        for b in range(NB):
            x = rhs[d][b]
            tail = None
            if b < NB - 1:
                tail = [jnp.broadcast_to(lane_sum(border_ref[j, b, 4 + a] * x), shape) for a in range(4)]
            head = [jnp.broadcast_to(lane_sum(border_ref[j, b, a] * x), shape) for a in range(4)]
            tails.append(tail)
            heads.append(head)
        for b in range(1, NB):
            prev = tails[b - 1]
            if b < NB - 1:
                tails[b] = [
                    tails[b][a] - sum(step_ref[j, b, 0, a, g] * prev[g] for g in range(4)) for a in range(4)
                ]
            heads[b] = [heads[b][a] - sum(step_ref[j, b, 1, a, g] * prev[g] for g in range(4)) for a in range(4)]
        for b in range(NB - 2, 0, -1):
            nxt = heads[b + 1]
            heads[b] = [heads[b][a] - sum(step_ref[j, b, 2, a, g] * nxt[g] for g in range(4)) for a in range(4)]
        for b in range(NB):
            x = rhs[d][b]
            lanes = slice(b * BK, (b + 1) * BK)
            if b > 0:
                x = x - sum(tails[b - 1][g] * below_ref[g : g + 1, lanes] for g in range(4))
            if b < NB - 1:
                x = x - sum(heads[b + 1][g] * above_ref[g : g + 1, lanes] for g in range(4))
            corrected[d][b] = x
    row = lax.broadcasted_iota(jnp.int32, (8, BK), 0)
    for b in range(NB):
        x = jnp.concatenate([corrected[0][b], corrected[1][b]], axis=0)
        high = x.astype(jnp.bfloat16)
        low = (x - high.astype(jnp.float32)).astype(jnp.bfloat16)
        left = jnp.concatenate([high, low], axis=0)
        total = [jnp.zeros((8, BK), jnp.float32), jnp.zeros((8, BK), jnp.float32)]
        for q in range(8):
            matrix = inv_ref[q // MC, j * MC + q % MC, b]
            product = lax.dot_general(
                left, matrix, (((1,), (1,)), ((), ())), preferred_element_type=jnp.float32
            )
            for d in range(2):
                value = product[d * 8 : d * 8 + 8] + product[16 + d * 8 : 24 + d * 8]
                total[d] = jnp.where(row == q, value, total[d])
        for d in range(2):
            out_ref[j, d, :, b * BK : (b + 1) * BK] = total[d]


def solve_kernel(rhs_ref, inv_ref, weights_ref, out_ref, below_ref, above_ref, border_ref, step_ref):
    below, above = coupling_rows(weights_ref[...])
    for g in range(4):
        below_ref[g : g + 1, :] = below[g]
        above_ref[g : g + 1, :] = above[g]

    @pl.loop(0, CHUNKS)
    def _(j):
        @pl.loop(0, NB)
        def _(b):
            prepare(inv_ref, below_ref, above_ref, border_ref, step_ref, j, b)

    @pl.loop(0, CHUNKS)
    def _(j):
        rhs = [[rhs_ref[j, d, :, b * BK : (b + 1) * BK] for b in range(NB)] for d in range(2)]
        solve_chunk(rhs, inv_ref, below_ref, above_ref, border_ref, step_ref, out_ref, j)


def block_solve(rhs, inverses, weights):
    return pl.pallas_call(
        solve_kernel,
        out_shape=jax.ShapeDtypeStruct((CHUNKS, 2, 8, NR), jnp.float32),
        in_specs=[pl.BlockSpec(memory_space=pltpu.VMEM)] * 3,
        out_specs=pl.BlockSpec(memory_space=pltpu.VMEM),
        scratch_shapes=[
            pltpu.VMEM((8, NR), jnp.float32),
            pltpu.VMEM((8, NR), jnp.float32),
            pltpu.VMEM((CHUNKS, NB, 8, 8, BK), jnp.float32),
            pltpu.VMEM((CHUNKS, NB, 3, 4, 4, 8, BK), jnp.float32),
        ],
        compiler_params=pltpu.CompilerParams(vmem_limit_bytes=48 * 2**20),
        name="block_solve",
    )(rhs, inverses, weights)


def explicit_terms(state, weights, radial_points, azimuth_index, wavenumber):
    length = state.shape[-1]
    padded = jnp.pad(state, [(0, 0)] * 3 + [(4, 4)])
    total = state
    for offset in range(9):
        total = total + weights[offset] * padded[..., offset : offset + length]
    shift = (azimuth_index[:, None, :, None] / MTH) ** 2 / radial_points**2 + AXIAL_FACTOR * wavenumber**2
    return total - shift * state


def body(forcing, spectral_state, block_inverses, second_weights, first_weights, radial_points):
    mode_devices = lax.axis_size("mode")
    mode_count = MTH // mode_devices
    azimuth_cols = jnp.asarray(azimuth_table())
    axial_cols = jnp.asarray(axial_table())
    spectra = jnp.einsum(
        "przt,tcm->pmczr", forcing, azimuth_cols, preferred_element_type=jnp.float32
    ).astype(jnp.bfloat16)
    combined = jnp.einsum(
        "pgmczr,czkd->pmkdr",
        lax.all_to_all(
            spectra.reshape(2, mode_devices, mode_count, 2, 4, BK),
            "mode",
            split_axis=1,
            concat_axis=4,
            tiled=True,
        ),
        axial_cols,
        preferred_element_type=jnp.float32,
    )
    regrouped = lax.all_to_all(combined, "rad", split_axis=2, concat_axis=4, tiled=True)
    index = lax.axis_index("mode") * mode_count + jnp.arange(mode_count, dtype=jnp.int32)
    index = jnp.broadcast_to(index.reshape(CHUNKS, 1, MC), (CHUNKS, 2, MC)).reshape(CHUNKS, 8)
    wavenumber = (lax.axis_index("rad") - KZ // 2).astype(jnp.float32)
    weights = second_weights + first_weights / radial_points

    def order(x):
        x = x.reshape(2, CHUNKS, MC, 2, NR)
        return x.transpose(1, 3, 0, 2, 4).reshape(CHUNKS, 2, 8, NR)

    rhs = explicit_terms(
        order(spectral_state), weights, radial_points, index.astype(jnp.float32), wavenumber
    ) + order(regrouped)
    out = block_solve(rhs, block_inverses.reshape(2, 16, NB, BK, BK), weights)
    out = out.reshape(CHUNKS, 2, 2, MC, NR).transpose(2, 0, 3, 1, 4)
    return out.reshape(2, mode_count, 1, 2, NR)


def solution(mesh):
    return jax.shard_map(
        body,
        mesh=mesh,
        in_specs=(
            P(None, "rad", "mode", None),
            P(None, "mode", "rad", None, None),
            P(None, "mode", "rad", None, None, None),
            P(),
            P(),
            P(),
        ),
        out_specs=P(None, "mode", "rad", None, None),
        check_vma=False,
    )
```

```python
import math

import jax
import jax.numpy as jnp
import numpy as np
from jax import lax
from jax.experimental import pallas as pl
from jax.experimental.pallas import tpu as pltpu
from jax.sharding import PartitionSpec as P

NTH = 1536
MTH = 512
NZ = 128
KZ = 8
BK = 128
NB = 8
NR = 1024
CHUNKS = 4
MC = 4


AXIAL_FACTOR = 0.05
MESH = pl.DeviceIdType.MESH


def azimuth_table():
    t = np.arange(NTH, dtype=np.int64)[:, None]
    m = np.arange(MTH, dtype=np.int64)[None, :]
    radians = 2.0 * math.pi / NTH * ((t * m) % NTH).astype(np.float64)
    norm = 1.0 / math.sqrt(NTH)
    table = np.stack([np.cos(radians) * norm, -np.sin(radians) * norm], axis=1)
    return table.astype(np.float32).astype(jnp.bfloat16)


def axial_table():
    z = np.arange(NZ, dtype=np.int64)[:, None]
    q = np.arange(KZ, dtype=np.int64)[None, :] - KZ // 2
    radians = 2.0 * math.pi / NZ * (((q % NZ) * z) % NZ).astype(np.float64)
    norm = 1.0 / math.sqrt(NZ)
    c = np.cos(radians) * norm
    s = np.sin(radians) * norm
    table = np.stack([np.stack([c, -s], axis=-1), np.stack([s, c], axis=-1)], axis=0)
    return table.astype(np.float32).astype(jnp.bfloat16)


def border_rows(inv_ref, j, b):
    per_problem = []
    for p in range(2):
        for i in range(MC):
            top = inv_ref[p, j * MC + i, b, 0:16, :].astype(jnp.float32)
            low = inv_ref[p, j * MC + i, b, BK - 16 : BK, :].astype(jnp.float32)
            per_problem.append(jnp.concatenate([top[0:4], low[12:16]], axis=0))
    return jnp.swapaxes(jnp.stack(per_problem, axis=0), 0, 1)


def coupling_rows(weights):
    place = lax.broadcasted_iota(jnp.int32, (1, NR), 1) % BK
    below, above = [], []
    for g in range(4):
        m = jnp.zeros((1, NR), jnp.float32)
        n = jnp.zeros((1, NR), jnp.float32)
        for a in range(4):
            if g >= a:
                m = jnp.where(place == a, -weights[g - a : g - a + 1, :], m)
            if g <= a:
                n = jnp.where(place == BK - 4 + a, -weights[g - a + 8 : g - a + 9, :], n)
        below.append(m)
        above.append(n)
    return below, above


def lane_sum(value):
    return jnp.sum(value, axis=-1, keepdims=True)


def prepare(inv_ref, below_ref, above_ref, border_ref, step_ref, j, b):
    rows = border_rows(inv_ref, j, b)
    border_ref[j, b] = rows
    lanes = pl.ds(pl.multiple_of(b * BK, BK), BK)
    for g in range(4):
        m = below_ref[g : g + 1, lanes]
        n = above_ref[g : g + 1, lanes]
        for a in range(4):
            shape = (8, BK)
            step_ref[j, b, 0, a, g] = jnp.broadcast_to(lane_sum(rows[4 + a] * m), shape)
            step_ref[j, b, 1, a, g] = jnp.broadcast_to(lane_sum(rows[a] * m), shape)
            step_ref[j, b, 2, a, g] = jnp.broadcast_to(lane_sum(rows[a] * n), shape)


def solve_chunk(rhs, inv_ref, below_ref, above_ref, border_ref, step_ref, out_ref, j):
    shape = (8, BK)
    corrected = [[None] * NB for _ in range(2)]
    for d in range(2):
        tails = []
        heads = []
        for b in range(NB):
            x = rhs[d][b]
            tail = None
            if b < NB - 1:
                tail = [jnp.broadcast_to(lane_sum(border_ref[j, b, 4 + a] * x), shape) for a in range(4)]
            head = [jnp.broadcast_to(lane_sum(border_ref[j, b, a] * x), shape) for a in range(4)]
            tails.append(tail)
            heads.append(head)
        for b in range(1, NB):
            prev = tails[b - 1]
            if b < NB - 1:
                tails[b] = [
                    tails[b][a] - sum(step_ref[j, b, 0, a, g] * prev[g] for g in range(4)) for a in range(4)
                ]
            heads[b] = [heads[b][a] - sum(step_ref[j, b, 1, a, g] * prev[g] for g in range(4)) for a in range(4)]
        for b in range(NB - 2, 0, -1):
            nxt = heads[b + 1]
            heads[b] = [heads[b][a] - sum(step_ref[j, b, 2, a, g] * nxt[g] for g in range(4)) for a in range(4)]
        for b in range(NB):
            x = rhs[d][b]
            lanes = slice(b * BK, (b + 1) * BK)
            if b > 0:
                x = x - sum(tails[b - 1][g] * below_ref[g : g + 1, lanes] for g in range(4))
            if b < NB - 1:
                x = x - sum(heads[b + 1][g] * above_ref[g : g + 1, lanes] for g in range(4))
            corrected[d][b] = x
    row = lax.broadcasted_iota(jnp.int32, (8, BK), 0)
    for b in range(NB):
        x = jnp.concatenate([corrected[0][b], corrected[1][b]], axis=0)
        high = x.astype(jnp.bfloat16)
        low = (x - high.astype(jnp.float32)).astype(jnp.bfloat16)
        left = jnp.concatenate([high, low], axis=0)
        total = [jnp.zeros((8, BK), jnp.float32), jnp.zeros((8, BK), jnp.float32)]
        for q in range(8):
            matrix = inv_ref[q // MC, j * MC + q % MC, b]
            product = lax.dot_general(
                left, matrix, (((1,), (1,)), ((), ())), preferred_element_type=jnp.float32
            )
            for d in range(2):
                value = product[d * 8 : d * 8 + 8] + product[16 + d * 8 : 24 + d * 8]
                total[d] = jnp.where(row == q, value, total[d])
        for d in range(2):
            out_ref[j, d, :, b * BK : (b + 1) * BK] = total[d]


def mode_order():
    order = []
    for j in range(CHUNKS):
        for h in range(2):
            for f in range(4):
                for s in range(4):
                    x, y = (f, s) if h == 0 else (s, f)
                    order += [((x * 4 + y) * 2 + h) * CHUNKS * MC + j * MC + i for i in range(MC)]
    return np.array(order)


def axial_blocks():
    table = axial_table().astype(np.float32)
    blocks = np.zeros((32, 4, KZ, 2, MC, 2, 2, 4, 4, MC), np.float32)
    for device in range(32):
        for source in range(2):
            first = (device ^ source) * 4
            part = table[:, first : first + 4].transpose(2, 3, 0, 1)
            for s in range(4):
                for i in range(MC):
                    blocks[device, s, :, :, i, source, :, :, s, i] = part
    return blocks.reshape(32, 256, 256).astype(jnp.bfloat16)


def whole_kernel(
    spectra_ref, explicit_ref, inv_ref, weights_ref, blocks_ref, out_ref,
    below_ref, above_ref, border_ref, step_ref, axial_ref, other_ref, part_ref, far_ref, near_ref,
    line_ref, far2_ref, near2_ref, total_ref, right_ref,
    axial_sem, swap_send, swap_recv, send_sem, recv_sem, rad_send, rad_recv,
):
    rad = lax.axis_index("rad")
    mode = lax.axis_index("mode")
    core = mode % 2
    y = (mode // 2) % 4
    x = mode // 8

    def device(xx, yy, cc, zz):
        return (zz, (xx * 4 + yy) * 2 + cc)

    load = pltpu.make_async_copy(blocks_ref.at[mode], axial_ref, axial_sem)
    load.start()

    barrier = pltpu.get_barrier_semaphore()
    sides = [((x + 1) % 4, y), ((x + 3) % 4, y), (x, (y + 1) % 4), (x, (y + 3) % 4)]
    for xx, yy in sides:
        pl.semaphore_signal(barrier, inc=1, device_id=device(xx, yy, core, rad), device_id_type=MESH)
    for dz in range(8):
        for cc in range(2):
            if dz or cc:
                pl.semaphore_signal(
                    barrier, inc=1, device_id=device(x, y, (core + cc) % 2, (rad + dz) % 8), device_id_type=MESH
                )
    pl.semaphore_wait(barrier, 19)

    def swap(j):
        return pltpu.make_async_remote_copy(
            src_ref=spectra_ref.at[1 - core, :, :, pl.ds(pl.multiple_of(j * 128, 128), 128), :],
            dst_ref=other_ref.at[j],
            send_sem=swap_send.at[j],
            recv_sem=swap_recv.at[j],
            device_id=device(x, y, 1 - core, rad),
            device_id_type=MESH,
        )

    for j in range(CHUNKS):
        swap(j).start()

    below, above = coupling_rows(weights_ref[...])
    for g in range(4):
        below_ref[g : g + 1, :] = below[g]
        above_ref[g : g + 1, :] = above[g]
    load.wait()

    first = (x, y)
    second = (y, x)

    def along(h, leg, step):
        if (h + leg) % 2 == 0:
            return device((x + step) % 4, y, core, rad)
        return device(x, (y + step) % 4, core, rad)

    def copy(j, h, i):
        f = first[h]
        s = second[h]
        leg = i // 6
        step = 1 if i % 2 == 0 else 3
        if i == 0:
            src, dst = part_ref.at[j, h, (f + 2) % 4, pl.ds(0, 2)], far_ref.at[j, h, 0]
        elif i == 1:
            src, dst = part_ref.at[j, h, (f + 2) % 4, pl.ds(2, 2)], far_ref.at[j, h, 1]
        elif i == 2:
            src, dst = part_ref.at[j, h, (f + 1) % 4, pl.ds(2, 2)], near_ref.at[j, h, 0, pl.ds(2, 2)]
        elif i == 3:
            src, dst = part_ref.at[j, h, (f + 3) % 4, pl.ds(0, 2)], near_ref.at[j, h, 1, pl.ds(0, 2)]
        elif i == 4:
            src, dst = part_ref.at[j, h, (f + 1) % 4, pl.ds(0, 2)], near_ref.at[j, h, 0, pl.ds(0, 2)]
        elif i == 5:
            src, dst = part_ref.at[j, h, (f + 3) % 4, pl.ds(2, 2)], near_ref.at[j, h, 1, pl.ds(2, 2)]
        elif i == 6:
            src, dst = line_ref.at[j, h, (s + 2) % 4, pl.ds(0, 32)], far2_ref.at[j, h, 0]
        elif i == 7:
            src, dst = line_ref.at[j, h, (s + 2) % 4, pl.ds(32, 32)], far2_ref.at[j, h, 1]
        elif i == 8:
            src, dst = line_ref.at[j, h, (s + 1) % 4, pl.ds(32, 32)], near2_ref.at[j, h, 0, pl.ds(32, 32)]
        elif i == 9:
            src, dst = line_ref.at[j, h, (s + 3) % 4, pl.ds(0, 32)], near2_ref.at[j, h, 1, pl.ds(0, 32)]
        elif i == 10:
            src, dst = line_ref.at[j, h, (s + 1) % 4, pl.ds(0, 32)], near2_ref.at[j, h, 0, pl.ds(0, 32)]
        else:
            src, dst = line_ref.at[j, h, (s + 3) % 4, pl.ds(32, 32)], near2_ref.at[j, h, 1, pl.ds(32, 32)]
        return pltpu.make_async_remote_copy(
            src_ref=src,
            dst_ref=dst,
            send_sem=send_sem.at[j, h, leg],
            recv_sem=recv_sem.at[j, h, i],
            device_id=along(h, leg, step),
            device_id_type=MESH,
        )

    def radial(j, h, dz):
        k = (rad + dz) % 8
        return pltpu.make_async_remote_copy(
            src_ref=total_ref.at[j, h, k],
            dst_ref=right_ref.at[j, rad * 2 + core],
            send_sem=rad_send.at[j, h],
            recv_sem=rad_recv.at[j],
            device_id=device(x, y, h, k),
            device_id_type=MESH,
        )

    def group(j, h, f):
        row = pl.ds(pl.multiple_of(j * 128 + h * 64 + f * 16, 16), 16)
        here = pl.ds(pl.multiple_of(h * 64 + f * 16, 16), 16)
        tiles = [spectra_ref[core, c, z, row, :] for c in range(2) for z in range(4)]
        tiles += [other_ref[j, c, z, here, :] for c in range(2) for z in range(4)]
        return jnp.concatenate(tiles, axis=0)

    def axial(j):
        swap(j).wait_recv()
        for pair in ((2, 1), (3, 0)):
            for h in range(2):
                f0 = (first[h] + pair[0]) % 4
                f1 = (first[h] + pair[1]) % 4
                right = jnp.concatenate([group(j, h, f0), group(j, h, f1)], axis=1)
                value = jnp.dot(axial_ref[...], right, preferred_element_type=jnp.float32).astype(jnp.bfloat16)
                part_ref[j, h, f0] = value[:, :BK].reshape(4, 64, BK)
                part_ref[j, h, f1] = value[:, BK:].reshape(4, 64, BK)
                for i in (0, 1, 2) if pair[0] == 2 else (3,):
                    copy(j, h, i).start()

    def add(a, b):
        return (a.astype(jnp.float32) + b.astype(jnp.float32)).astype(jnp.bfloat16)

    def relay(j):
        for h in range(2):
            plus = (first[h] + 1) % 4
            minus = (first[h] + 3) % 4
            copy(j, h, 0).wait_recv()
            part_ref[j, h, plus, 0:2] = add(part_ref[j, h, plus, 0:2], far_ref[j, h, 0])
            copy(j, h, 4).start()
            copy(j, h, 1).wait_recv()
            part_ref[j, h, minus, 2:4] = add(part_ref[j, h, minus, 2:4], far_ref[j, h, 1])
            copy(j, h, 5).start()

    def gather_line(j):
        for h in range(2):
            for i in (2, 3, 4, 5):
                copy(j, h, i).wait_recv()
            value = part_ref[j, h, first[h]].astype(jnp.float32)
            value = value + near_ref[j, h, 0].astype(jnp.float32) + near_ref[j, h, 1].astype(jnp.float32)
            line_ref[j, h] = value.astype(jnp.bfloat16)
            for i in (6, 7, 8, 9):
                copy(j, h, i).start()

    def relay_line(j):
        for h in range(2):
            plus = (second[h] + 1) % 4
            minus = (second[h] + 3) % 4
            copy(j, h, 6).wait_recv()
            line_ref[j, h, plus, 0:32] = add(line_ref[j, h, plus, 0:32], far2_ref[j, h, 0])
            copy(j, h, 10).start()
            copy(j, h, 7).wait_recv()
            line_ref[j, h, minus, 32:64] = add(line_ref[j, h, minus, 32:64], far2_ref[j, h, 1])
            copy(j, h, 11).start()

    def spread(j):
        for h in range(2):
            for i in (8, 9, 10, 11):
                copy(j, h, i).wait_recv()
            value = line_ref[j, h, second[h]].astype(jnp.float32)
            value = value + near2_ref[j, h, 0].astype(jnp.float32) + near2_ref[j, h, 1].astype(jnp.float32)
            total_ref[j, h] = value.reshape(8, 8, BK)
            for dz in range(1, 8):
                radial(j, h, dz).start()

            @pl.when(core == h)
            def _():
                right_ref[j, rad * 2 + core] = total_ref[j, h, rad]

            @pl.when(core != h)
            def _():
                radial(j, h, 0).start()

    def finish(j):
        arrived = right_ref.at[j, pl.ds(0, 15)]
        pltpu.make_async_copy(arrived, arrived, rad_recv.at[j]).wait()
        rhs = []
        for d in range(2):
            row = slice(4 * d, 4 * d + 4)
            rhs.append(
                [
                    jnp.concatenate([right_ref[j, 2 * b, row, :], right_ref[j, 2 * b + 1, row, :]], axis=0)
                    + explicit_ref[j, d, :, b * BK : (b + 1) * BK]
                    for b in range(NB)
                ]
            )
        solve_chunk(rhs, inv_ref, below_ref, above_ref, border_ref, step_ref, out_ref, j)
        swap(j).wait_send()
        for h in range(2):
            whole = part_ref.at[j, h, pl.ds(0, 3)]
            pltpu.make_async_copy(whole, whole, send_sem.at[j, h, 0]).wait()
            whole = line_ref.at[j, h, pl.ds(0, 3)]
            pltpu.make_async_copy(whole, whole, send_sem.at[j, h, 1]).wait()

            @pl.when(core == h)
            def _():
                whole = total_ref.at[j, h, pl.ds(0, 7)]
                pltpu.make_async_copy(whole, whole, rad_send.at[j, h]).wait()

            @pl.when(core != h)
            def _():
                whole = total_ref.at[j, h]
                pltpu.make_async_copy(whole, whole, rad_send.at[j, h]).wait()

    stages = [axial, relay, gather_line, relay_line, spread, finish]

    @pl.loop(0, CHUNKS + len(stages) - 1)
    def _(tick):
        for index, stage in enumerate(stages):
            j = tick - index

            @pl.when((j >= 0) & (j < CHUNKS))
            def _():
                stage(j)
                if index == 0:

                    @pl.loop(0, NB)
                    def _(b):
                        prepare(inv_ref, below_ref, above_ref, border_ref, step_ref, j, b)


def transform_and_solve(spectra, explicit, inverses, weights, blocks):
    bf16 = jnp.bfloat16
    tile = (CHUNKS, 2)
    vmem = pl.BlockSpec(memory_space=pltpu.VMEM)
    return pl.pallas_call(
        whole_kernel,
        out_shape=jax.ShapeDtypeStruct((CHUNKS, 2, 8, NR), jnp.float32),
        in_specs=[vmem, vmem, vmem, vmem, pl.BlockSpec(memory_space=pl.ANY)],
        out_specs=vmem,
        scratch_shapes=[
            pltpu.VMEM((8, NR), jnp.float32),
            pltpu.VMEM((8, NR), jnp.float32),
            pltpu.VMEM((CHUNKS, NB, 8, 8, BK), jnp.float32),
            pltpu.VMEM((CHUNKS, NB, 3, 4, 4, 8, BK), jnp.float32),
            pltpu.VMEM((256, 256), bf16),
            pltpu.VMEM((CHUNKS, 2, 4, 128, BK), bf16),
            pltpu.VMEM(tile + (4, 4, 64, BK), bf16),
            pltpu.VMEM(tile + (2, 2, 64, BK), bf16),
            pltpu.VMEM(tile + (2, 4, 64, BK), bf16),
            pltpu.VMEM(tile + (4, 64, BK), bf16),
            pltpu.VMEM(tile + (2, 32, BK), bf16),
            pltpu.VMEM(tile + (2, 64, BK), bf16),
            pltpu.VMEM(tile + (8, 8, BK), jnp.float32),
            pltpu.VMEM((CHUNKS, 16, 8, BK), jnp.float32),
            pltpu.SemaphoreType.DMA,
            pltpu.SemaphoreType.DMA((CHUNKS,)),
            pltpu.SemaphoreType.DMA((CHUNKS,)),
            pltpu.SemaphoreType.DMA((CHUNKS, 2, 2)),
            pltpu.SemaphoreType.DMA((CHUNKS, 2, 12)),
            pltpu.SemaphoreType.DMA((CHUNKS, 2)),
            pltpu.SemaphoreType.DMA((CHUNKS,)),
        ],
        compiler_params=pltpu.CompilerParams(
            vmem_limit_bytes=32 * 2**20, collective_id=0, has_side_effects=True
        ),
        name="transform_and_solve",
    )(spectra, explicit, inverses, weights, blocks)


def explicit_terms(state, weights, radial_points, azimuth_index, wavenumber):
    length = state.shape[-1]
    padded = jnp.pad(state, [(0, 0)] * 3 + [(4, 4)])
    total = state
    for offset in range(9):
        total = total + weights[offset] * padded[..., offset : offset + length]
    shift = (azimuth_index[:, None, :, None] / MTH) ** 2 / radial_points**2 + AXIAL_FACTOR * wavenumber**2
    return total - shift * state


def body(forcing, spectral_state, block_inverses, second_weights, first_weights, radial_points):
    mode_count = MTH // lax.axis_size("mode")
    azimuth_cols = jnp.asarray(azimuth_table()[:, :, mode_order()])
    blocks = jnp.asarray(axial_blocks())
    spectra = jnp.einsum(
        "przt,tcm->pczmr", forcing, azimuth_cols, preferred_element_type=jnp.float32
    ).astype(jnp.bfloat16)
    index = lax.axis_index("mode") * mode_count + jnp.arange(mode_count, dtype=jnp.int32)
    index = jnp.broadcast_to(index.reshape(CHUNKS, 1, MC), (CHUNKS, 2, MC)).reshape(CHUNKS, 8)
    wavenumber = (lax.axis_index("rad") - KZ // 2).astype(jnp.float32)
    weights = second_weights + first_weights / radial_points
    state = spectral_state.reshape(2, CHUNKS, MC, 2, NR).transpose(1, 3, 0, 2, 4).reshape(CHUNKS, 2, 8, NR)
    explicit = explicit_terms(state, weights, radial_points, index.astype(jnp.float32), wavenumber)
    out = transform_and_solve(
        spectra, explicit, block_inverses.reshape(2, mode_count, NB, BK, BK), weights, blocks
    )
    out = out.reshape(CHUNKS, 2, 2, MC, NR).transpose(2, 0, 3, 1, 4)
    return out.reshape(2, mode_count, 1, 2, NR)


def solution(mesh):
    return jax.shard_map(
        body,
        mesh=mesh,
        in_specs=(
            P(None, "rad", "mode", None),
            P(None, "mode", "rad", None, None),
            P(None, "mode", "rad", None, None, None),
            P(),
            P(),
            P(),
        ),
        out_specs=P(None, "mode", "rad", None, None),
        check_vma=False,
    )
```

```python
import math

import jax
import jax.numpy as jnp
import numpy as np
from jax import lax
from jax.experimental import pallas as pl
from jax.experimental.pallas import tpu as pltpu
from jax.sharding import PartitionSpec as P

NTH = 1536
MTH = 512
NZ = 128
KZ = 8
BK = 128
NB = 8
NR = 1024
CHUNKS = 4
MC = 4


AXIAL_FACTOR = 0.05
MESH = pl.DeviceIdType.MESH


def azimuth_table():
    t = np.arange(NTH, dtype=np.int64)[:, None]
    m = np.arange(MTH, dtype=np.int64)[None, :]
    radians = 2.0 * math.pi / NTH * ((t * m) % NTH).astype(np.float64)
    norm = 1.0 / math.sqrt(NTH)
    table = np.stack([np.cos(radians) * norm, -np.sin(radians) * norm], axis=1)
    return table.astype(np.float32).astype(jnp.bfloat16)


def axial_table():
    z = np.arange(NZ, dtype=np.int64)[:, None]
    q = np.arange(KZ, dtype=np.int64)[None, :] - KZ // 2
    radians = 2.0 * math.pi / NZ * (((q % NZ) * z) % NZ).astype(np.float64)
    norm = 1.0 / math.sqrt(NZ)
    c = np.cos(radians) * norm
    s = np.sin(radians) * norm
    table = np.stack([np.stack([c, -s], axis=-1), np.stack([s, c], axis=-1)], axis=0)
    return table.astype(np.float32).astype(jnp.bfloat16)


def border_rows(inv_ref, j, b):
    per_problem = []
    for p in range(2):
        for i in range(MC):
            top = inv_ref[p, j * MC + i, b, 0:16, :].astype(jnp.float32)
            low = inv_ref[p, j * MC + i, b, BK - 16 : BK, :].astype(jnp.float32)
            per_problem.append(jnp.concatenate([top[0:4], low[12:16]], axis=0))
    return jnp.swapaxes(jnp.stack(per_problem, axis=0), 0, 1)


def coupling_rows(weights):
    place = lax.broadcasted_iota(jnp.int32, (1, NR), 1) % BK
    below, above = [], []
    for g in range(4):
        m = jnp.zeros((1, NR), jnp.float32)
        n = jnp.zeros((1, NR), jnp.float32)
        for a in range(4):
            if g >= a:
                m = jnp.where(place == a, -weights[g - a : g - a + 1, :], m)
            if g <= a:
                n = jnp.where(place == BK - 4 + a, -weights[g - a + 8 : g - a + 9, :], n)
        below.append(m)
        above.append(n)
    return below, above


def lane_sum(value):
    return jnp.sum(value, axis=-1, keepdims=True)


def prepare(inv_ref, below_ref, above_ref, border_ref, step_ref, j, b):
    rows = border_rows(inv_ref, j, b)
    border_ref[j, b] = rows
    lanes = pl.ds(pl.multiple_of(b * BK, BK), BK)
    for g in range(4):
        m = below_ref[g : g + 1, lanes]
        n = above_ref[g : g + 1, lanes]
        for a in range(4):
            shape = (8, BK)
            step_ref[j, b, 0, a, g] = jnp.broadcast_to(lane_sum(rows[4 + a] * m), shape)
            step_ref[j, b, 1, a, g] = jnp.broadcast_to(lane_sum(rows[a] * m), shape)
            step_ref[j, b, 2, a, g] = jnp.broadcast_to(lane_sum(rows[a] * n), shape)


def solve_chunk(rhs, inv_ref, below_ref, above_ref, border_ref, step_ref, out_ref, j):
    shape = (8, BK)
    corrected = [[None] * NB for _ in range(2)]
    for d in range(2):
        tails = []
        heads = []
        for b in range(NB):
            x = rhs[d][b]
            tail = None
            if b < NB - 1:
                tail = [jnp.broadcast_to(lane_sum(border_ref[j, b, 4 + a] * x), shape) for a in range(4)]
            head = [jnp.broadcast_to(lane_sum(border_ref[j, b, a] * x), shape) for a in range(4)]
            tails.append(tail)
            heads.append(head)
        for b in range(1, NB):
            prev = tails[b - 1]
            if b < NB - 1:
                tails[b] = [
                    tails[b][a] - sum(step_ref[j, b, 0, a, g] * prev[g] for g in range(4)) for a in range(4)
                ]
            heads[b] = [heads[b][a] - sum(step_ref[j, b, 1, a, g] * prev[g] for g in range(4)) for a in range(4)]
        for b in range(NB - 2, 0, -1):
            nxt = heads[b + 1]
            heads[b] = [heads[b][a] - sum(step_ref[j, b, 2, a, g] * nxt[g] for g in range(4)) for a in range(4)]
        for b in range(NB):
            x = rhs[d][b]
            lanes = slice(b * BK, (b + 1) * BK)
            if b > 0:
                x = x - sum(tails[b - 1][g] * below_ref[g : g + 1, lanes] for g in range(4))
            if b < NB - 1:
                x = x - sum(heads[b + 1][g] * above_ref[g : g + 1, lanes] for g in range(4))
            corrected[d][b] = x
    row = lax.broadcasted_iota(jnp.int32, (8, BK), 0)
    for b in range(NB):
        x = jnp.concatenate([corrected[0][b], corrected[1][b]], axis=0)
        high = x.astype(jnp.bfloat16)
        low = (x - high.astype(jnp.float32)).astype(jnp.bfloat16)
        left = jnp.concatenate([high, low], axis=0)
        total = [jnp.zeros((8, BK), jnp.float32), jnp.zeros((8, BK), jnp.float32)]
        for q in range(8):
            matrix = inv_ref[q // MC, j * MC + q % MC, b]
            product = lax.dot_general(
                left, matrix, (((1,), (1,)), ((), ())), preferred_element_type=jnp.float32
            )
            for d in range(2):
                value = product[d * 8 : d * 8 + 8] + product[16 + d * 8 : 24 + d * 8]
                total[d] = jnp.where(row == q, value, total[d])
        for d in range(2):
            for q in range(8):
                out_ref[q // MC, j * MC + q % MC, d : d + 1, b * BK : (b + 1) * BK] = total[d][q : q + 1]


def mode_order():
    order = []
    for j in range(CHUNKS):
        for h in range(2):
            for f in range(4):
                for s in range(4):
                    x, y = (f, s) if h == 0 else (s, f)
                    order += [((x * 4 + y) * 2 + h) * CHUNKS * MC + j * MC + i for i in range(MC)]
    return np.array(order)


def axial_blocks():
    table = axial_table().astype(np.float32)
    blocks = np.zeros((32, KZ, 2, MC, 2, 2, 4, 4, MC), np.float32)
    for device in range(32):
        for source in range(2):
            first = (device ^ source) * 4
            part = table[:, first : first + 4].transpose(2, 3, 0, 1)
            for s in range(4):
                for i in range(MC):
                    blocks[device, :, :, i, source, :, :, s, i] = part
    return blocks.reshape(32, 64, 256)


def whole_kernel(
    spectra_ref, state_ref, inv_ref, second_ref, first_ref, points_ref, blocks_ref, out_ref,
    weights_ref, explicit_ref, below_ref, above_ref, border_ref, step_ref, block_ref, axial_ref, other_ref, part_ref,
    far_ref, near_ref, line_ref, near2_ref, total_ref, right_ref,
    axial_sem, swap_send, swap_recv, send_sem, recv_sem, rad_send, rad_recv,
):
    rad = lax.axis_index("rad")
    mode = lax.axis_index("mode")
    core = mode % 2
    y = (mode // 2) % 4
    x = mode // 8

    def device(xx, yy, cc, zz):
        return (zz, (xx * 4 + yy) * 2 + cc)

    load = pltpu.make_async_copy(blocks_ref.at[mode], block_ref, axial_sem)
    load.start()

    barrier = pltpu.get_barrier_semaphore()
    sides = [((x + 1) % 4, y), ((x + 3) % 4, y), (x, (y + 1) % 4), (x, (y + 3) % 4)]
    for xx, yy in sides:
        pl.semaphore_signal(barrier, inc=1, device_id=device(xx, yy, core, rad), device_id_type=MESH)
    for dz in range(8):
        for cc in range(2):
            if dz or cc:
                pl.semaphore_signal(
                    barrier, inc=1, device_id=device(x, y, (core + cc) % 2, (rad + dz) % 8), device_id_type=MESH
                )
    pl.semaphore_wait(barrier, 19)

    def swap(j):
        return pltpu.make_async_remote_copy(
            src_ref=spectra_ref.at[1 - core, :, :, pl.ds(pl.multiple_of(j * 128, 128), 128), :],
            dst_ref=other_ref.at[j],
            send_sem=swap_send.at[j],
            recv_sem=swap_recv.at[j],
            device_id=device(x, y, 1 - core, rad),
            device_id_type=MESH,
        )

    for j in range(CHUNKS):
        swap(j).start()

    points = points_ref[...]
    weights = second_ref[...] + first_ref[...] / points
    weights_ref[...] = weights
    below, above = coupling_rows(weights)
    for g in range(4):
        below_ref[g : g + 1, :] = below[g]
        above_ref[g : g + 1, :] = above[g]
    load.wait()
    place = lax.broadcasted_iota(jnp.int32, (64, 256), 1) // MC % 4
    for s in range(4):
        axial_ref[64 * s : 64 * s + 64] = jnp.where(place == s, block_ref[...], 0.0).astype(jnp.bfloat16)

    first = (x, y)
    second = (y, x)

    def along(h, leg, step):
        if (h + leg) % 2 == 0:
            return device((x + step) % 4, y, core, rad)
        return device(x, (y + step) % 4, core, rad)

    def copy(j, h, i):
        f = first[h]
        s = second[h]
        leg = i // 6
        step = (1 if i % 2 == 0 else 3) if i < 6 else i - 5
        if i == 0:
            src, dst = part_ref.at[j, h, (f + 2) % 4, pl.ds(0, 2)], far_ref.at[j, h, 0]
        elif i == 1:
            src, dst = part_ref.at[j, h, (f + 2) % 4, pl.ds(2, 2)], far_ref.at[j, h, 1]
        elif i == 2:
            src, dst = part_ref.at[j, h, (f + 1) % 4, pl.ds(2, 2)], near_ref.at[j, h, 0, pl.ds(2, 2)]
        elif i == 3:
            src, dst = part_ref.at[j, h, (f + 3) % 4, pl.ds(0, 2)], near_ref.at[j, h, 1, pl.ds(0, 2)]
        elif i == 4:
            src, dst = part_ref.at[j, h, (f + 1) % 4, pl.ds(0, 2)], near_ref.at[j, h, 0, pl.ds(0, 2)]
        elif i == 5:
            src, dst = part_ref.at[j, h, (f + 3) % 4, pl.ds(2, 2)], near_ref.at[j, h, 1, pl.ds(2, 2)]
        else:
            src, dst = line_ref.at[j, h, (s + i - 5) % 4], near2_ref.at[j, h, i - 6]
        return pltpu.make_async_remote_copy(
            src_ref=src,
            dst_ref=dst,
            send_sem=send_sem.at[j, h, leg],
            recv_sem=recv_sem.at[j, h, i],
            device_id=along(h, leg, step),
            device_id_type=MESH,
        )

    def radial(j, h, dz):
        k = (rad + dz) % 8
        return pltpu.make_async_remote_copy(
            src_ref=total_ref.at[j, h, k],
            dst_ref=right_ref.at[j, rad * 2 + core],
            send_sem=rad_send.at[j, h],
            recv_sem=rad_recv.at[j],
            device_id=device(x, y, h, k),
            device_id_type=MESH,
        )

    def group(j, h, f):
        row = pl.ds(pl.multiple_of(j * 128 + h * 64 + f * 16, 16), 16)
        here = pl.ds(pl.multiple_of(h * 64 + f * 16, 16), 16)
        tiles = [spectra_ref[core, c, z, row, :] for c in range(2) for z in range(4)]
        tiles += [other_ref[j, c, z, here, :] for c in range(2) for z in range(4)]
        return jnp.concatenate(tiles, axis=0)

    def axial(j):
        swap(j).wait_recv()
        for pair in ((2, 1), (3, 0)):
            for h in range(2):
                f0 = (first[h] + pair[0]) % 4
                f1 = (first[h] + pair[1]) % 4
                right = jnp.concatenate([group(j, h, f0), group(j, h, f1)], axis=1)
                value = jnp.dot(axial_ref[...], right, preferred_element_type=jnp.float32).astype(jnp.bfloat16)
                part_ref[j, h, f0] = value[:, :BK].reshape(4, 64, BK)
                part_ref[j, h, f1] = value[:, BK:].reshape(4, 64, BK)
                for i in (0, 1, 2) if pair[0] == 2 else (3,):
                    copy(j, h, i).start()

    def explicit(j):
        inverse_square = 1.0 / (points_ref[...] * points_ref[...])
        row = lax.broadcasted_iota(jnp.int32, (8, 1), 0)
        index = (mode * CHUNKS * MC + j * MC + row % MC).astype(jnp.float32) * (1.0 / MTH)
        wave = (rad - KZ // 2).astype(jnp.float32)
        shift = index * index * inverse_square + AXIAL_FACTOR * (wave * wave)
        zeros = jnp.zeros((8, BK), jnp.float32)
        for d in range(2):
            state = jnp.concatenate(
                [state_ref[p, j * MC + i, d : d + 1, :] for p in range(2) for i in range(MC)], axis=0
            )
            padded = jnp.concatenate([zeros, state, zeros], axis=1)
            value = state - shift * state
            for o in range(9):
                value = value + weights_ref[o : o + 1, :] * padded[:, BK - 4 + o : BK - 4 + o + NR]
            explicit_ref[j, d] = value

    def add(a, b):
        return (a.astype(jnp.float32) + b.astype(jnp.float32)).astype(jnp.bfloat16)

    def relay(j):
        for h in range(2):
            plus = (first[h] + 1) % 4
            minus = (first[h] + 3) % 4
            copy(j, h, 0).wait_recv()
            part_ref[j, h, plus, 0:2] = add(part_ref[j, h, plus, 0:2], far_ref[j, h, 0])
            copy(j, h, 4).start()
            copy(j, h, 1).wait_recv()
            part_ref[j, h, minus, 2:4] = add(part_ref[j, h, minus, 2:4], far_ref[j, h, 1])
            copy(j, h, 5).start()

    def gather_line(j):
        for h in range(2):
            for i in (2, 3, 4, 5):
                copy(j, h, i).wait_recv()
            value = part_ref[j, h, first[h]].astype(jnp.float32)
            value = value + near_ref[j, h, 0].astype(jnp.float32) + near_ref[j, h, 1].astype(jnp.float32)
            line_ref[j, h] = value.astype(jnp.bfloat16)
            for i in (7, 6, 8):
                copy(j, h, i).start()

    def spread(j):
        for h in range(2):
            for i in (6, 7, 8):
                copy(j, h, i).wait_recv()
            value = line_ref[j, h, second[h]].astype(jnp.float32)
            for i in range(3):
                value = value + near2_ref[j, h, i].astype(jnp.float32)
            total_ref[j, h] = value.astype(jnp.bfloat16).reshape(8, 8, BK)
            for dz in (4, 3, 5, 2, 6, 1, 7):
                radial(j, h, dz).start()

            @pl.when(core == h)
            def _():
                right_ref[j, rad * 2 + core] = total_ref[j, h, rad]

            @pl.when(core != h)
            def _():
                radial(j, h, 0).start()

    def finish(j):
        arrived = right_ref.at[j, pl.ds(0, 15)]
        pltpu.make_async_copy(arrived, arrived, rad_recv.at[j]).wait()
        arrival = [right_ref[j, i].astype(jnp.float32) for i in range(16)]
        rhs = []
        for d in range(2):
            row = slice(4 * d, 4 * d + 4)
            rhs.append(
                [
                    jnp.concatenate([arrival[2 * b][row], arrival[2 * b + 1][row]], axis=0)
                    + explicit_ref[j, d, :, b * BK : (b + 1) * BK]
                    for b in range(NB)
                ]
            )
        solve_chunk(rhs, inv_ref, below_ref, above_ref, border_ref, step_ref, out_ref, j)
        swap(j).wait_send()
        for h in range(2):
            whole = part_ref.at[j, h, pl.ds(0, 3)]
            pltpu.make_async_copy(whole, whole, send_sem.at[j, h, 0]).wait()
            whole = line_ref.at[j, h, pl.ds(0, 3)]
            pltpu.make_async_copy(whole, whole, send_sem.at[j, h, 1]).wait()

            @pl.when(core == h)
            def _():
                whole = total_ref.at[j, h, pl.ds(0, 7)]
                pltpu.make_async_copy(whole, whole, rad_send.at[j, h]).wait()

            @pl.when(core != h)
            def _():
                whole = total_ref.at[j, h]
                pltpu.make_async_copy(whole, whole, rad_send.at[j, h]).wait()

    stages = [axial, relay, gather_line, spread, finish]

    @pl.loop(0, CHUNKS + len(stages) - 1)
    def _(tick):
        for index, stage in enumerate(stages):
            j = tick - index

            @pl.when((j >= 0) & (j < CHUNKS))
            def _():
                stage(j)
                if index == 0:
                    explicit(j)

                    @pl.loop(0, NB)
                    def _(b):
                        prepare(inv_ref, below_ref, above_ref, border_ref, step_ref, j, b)


def transform_and_solve(spectra, state, inverses, second_weights, first_weights, points, blocks):
    bf16 = jnp.bfloat16
    tile = (CHUNKS, 2)
    vmem = pl.BlockSpec(memory_space=pltpu.VMEM)
    return pl.pallas_call(
        whole_kernel,
        out_shape=jax.ShapeDtypeStruct(state.shape, jnp.float32),
        in_specs=[vmem] * 6 + [pl.BlockSpec(memory_space=pl.ANY)],
        out_specs=vmem,
        scratch_shapes=[
            pltpu.VMEM((9, NR), jnp.float32),
            pltpu.VMEM((CHUNKS, 2, 8, NR), jnp.float32),
            pltpu.VMEM((8, NR), jnp.float32),
            pltpu.VMEM((8, NR), jnp.float32),
            pltpu.VMEM((CHUNKS, NB, 8, 8, BK), jnp.float32),
            pltpu.VMEM((CHUNKS, NB, 3, 4, 4, 8, BK), jnp.float32),
            pltpu.VMEM((64, 256), jnp.float32),
            pltpu.VMEM((256, 256), bf16),
            pltpu.VMEM((CHUNKS, 2, 4, 128, BK), bf16),
            pltpu.VMEM(tile + (4, 4, 64, BK), bf16),
            pltpu.VMEM(tile + (2, 2, 64, BK), bf16),
            pltpu.VMEM(tile + (2, 4, 64, BK), bf16),
            pltpu.VMEM(tile + (4, 64, BK), bf16),
            pltpu.VMEM(tile + (3, 64, BK), bf16),
            pltpu.VMEM(tile + (8, 8, BK), bf16),
            pltpu.VMEM((CHUNKS, 16, 8, BK), bf16),
            pltpu.SemaphoreType.DMA,
            pltpu.SemaphoreType.DMA((CHUNKS,)),
            pltpu.SemaphoreType.DMA((CHUNKS,)),
            pltpu.SemaphoreType.DMA((CHUNKS, 2, 2)),
            pltpu.SemaphoreType.DMA((CHUNKS, 2, 9)),
            pltpu.SemaphoreType.DMA((CHUNKS, 2)),
            pltpu.SemaphoreType.DMA((CHUNKS,)),
        ],
        compiler_params=pltpu.CompilerParams(
            vmem_limit_bytes=32 * 2**20, collective_id=0, has_side_effects=True
        ),
        name="transform_and_solve",
    )(spectra, state, inverses, second_weights, first_weights, points, blocks)


def body(forcing, spectral_state, block_inverses, second_weights, first_weights, radial_points):
    mode_count = MTH // lax.axis_size("mode")
    azimuth_cols = jnp.asarray(azimuth_table()[:, :, mode_order()])
    blocks = jnp.asarray(axial_blocks())
    spectra = jnp.einsum(
        "przt,tcm->pczmr", forcing, azimuth_cols, preferred_element_type=jnp.float32
    ).astype(jnp.bfloat16)
    out = transform_and_solve(
        spectra,
        spectral_state.reshape(2, mode_count, 2, NR),
        block_inverses.reshape(2, mode_count, NB, BK, BK),
        second_weights,
        first_weights,
        radial_points.reshape(1, NR),
        blocks,
    )
    return out.reshape(2, mode_count, 1, 2, NR)


def solution(mesh):
    return jax.shard_map(
        body,
        mesh=mesh,
        in_specs=(
            P(None, "rad", "mode", None),
            P(None, "mode", "rad", None, None),
            P(None, "mode", "rad", None, None, None),
            P(),
            P(),
            P(),
        ),
        out_specs=P(None, "mode", "rad", None, None),
        check_vma=False,
    )
```

```python
import math

import jax
import jax.numpy as jnp
import numpy as np
from jax import lax
from jax.experimental import pallas as pl
from jax.experimental.pallas import tpu as pltpu
from jax.sharding import PartitionSpec as P

NTH = 1536
MTH = 512
NZ = 128
KZ = 8
BK = 128
NB = 8
NR = 1024
CHUNKS = 4
MC = 4


AXIAL_FACTOR = 0.05
MESH = pl.DeviceIdType.MESH


def azimuth_table():
    t = np.arange(NTH, dtype=np.int64)[:, None]
    m = np.arange(MTH, dtype=np.int64)[None, :]
    radians = 2.0 * math.pi / NTH * ((t * m) % NTH).astype(np.float64)
    norm = 1.0 / math.sqrt(NTH)
    table = np.stack([np.cos(radians) * norm, -np.sin(radians) * norm], axis=1)
    return table.astype(np.float32).astype(jnp.bfloat16)


def axial_table():
    z = np.arange(NZ, dtype=np.int64)[:, None]
    q = np.arange(KZ, dtype=np.int64)[None, :] - KZ // 2
    radians = 2.0 * math.pi / NZ * (((q % NZ) * z) % NZ).astype(np.float64)
    norm = 1.0 / math.sqrt(NZ)
    c = np.cos(radians) * norm
    s = np.sin(radians) * norm
    table = np.stack([np.stack([c, -s], axis=-1), np.stack([s, c], axis=-1)], axis=0)
    return table.astype(np.float32).astype(jnp.bfloat16)


def border_rows(inv_ref, j, b):
    per_problem = []
    for p in range(2):
        for i in range(MC):
            top = inv_ref[p, j * MC + i, b, 0:16, :].astype(jnp.float32)
            low = inv_ref[p, j * MC + i, b, BK - 16 : BK, :].astype(jnp.float32)
            per_problem.append(jnp.concatenate([top[0:4], low[12:16]], axis=0))
    return jnp.swapaxes(jnp.stack(per_problem, axis=0), 0, 1)


def coupling_rows(weights):
    place = lax.broadcasted_iota(jnp.int32, (1, NR), 1) % BK
    below, above = [], []
    for g in range(4):
        m = jnp.zeros((1, NR), jnp.float32)
        n = jnp.zeros((1, NR), jnp.float32)
        for a in range(4):
            if g >= a:
                m = jnp.where(place == a, -weights[g - a : g - a + 1, :], m)
            if g <= a:
                n = jnp.where(place == BK - 4 + a, -weights[g - a + 8 : g - a + 9, :], n)
        below.append(m)
        above.append(n)
    return below, above


def lane_sum(value):
    return jnp.sum(value, axis=-1, keepdims=True)


def prepare(inv_ref, below_ref, above_ref, border_ref, step_ref, j, b):
    rows = border_rows(inv_ref, j, b)
    border_ref[j, b] = rows
    lanes = pl.ds(pl.multiple_of(b * BK, BK), BK)
    for g in range(4):
        m = below_ref[g : g + 1, lanes]
        n = above_ref[g : g + 1, lanes]
        for a in range(4):
            shape = (8, BK)
            step_ref[j, b, 0, a, g] = jnp.broadcast_to(lane_sum(rows[4 + a] * m), shape)
            step_ref[j, b, 1, a, g] = jnp.broadcast_to(lane_sum(rows[a] * m), shape)
            step_ref[j, b, 2, a, g] = jnp.broadcast_to(lane_sum(rows[a] * n), shape)


def solve_chunk(rhs, inv_ref, below_ref, above_ref, border_ref, step_ref, out_ref, j):
    shape = (8, BK)
    corrected = [[None] * NB for _ in range(2)]
    for d in range(2):
        tails = []
        heads = []
        for b in range(NB):
            x = rhs[d][b]
            tail = None
            if b < NB - 1:
                tail = [jnp.broadcast_to(lane_sum(border_ref[j, b, 4 + a] * x), shape) for a in range(4)]
            head = [jnp.broadcast_to(lane_sum(border_ref[j, b, a] * x), shape) for a in range(4)]
            tails.append(tail)
            heads.append(head)
        for b in range(1, NB):
            prev = tails[b - 1]
            if b < NB - 1:
                tails[b] = [
                    tails[b][a] - sum(step_ref[j, b, 0, a, g] * prev[g] for g in range(4)) for a in range(4)
                ]
            heads[b] = [heads[b][a] - sum(step_ref[j, b, 1, a, g] * prev[g] for g in range(4)) for a in range(4)]
        for b in range(NB - 2, 0, -1):
            nxt = heads[b + 1]
            heads[b] = [heads[b][a] - sum(step_ref[j, b, 2, a, g] * nxt[g] for g in range(4)) for a in range(4)]
        for b in range(NB):
            x = rhs[d][b]
            lanes = slice(b * BK, (b + 1) * BK)
            if b > 0:
                x = x - sum(tails[b - 1][g] * below_ref[g : g + 1, lanes] for g in range(4))
            if b < NB - 1:
                x = x - sum(heads[b + 1][g] * above_ref[g : g + 1, lanes] for g in range(4))
            corrected[d][b] = x
    row = lax.broadcasted_iota(jnp.int32, (8, BK), 0)
    for b in range(NB):
        x = jnp.concatenate([corrected[0][b], corrected[1][b]], axis=0)
        high = x.astype(jnp.bfloat16)
        low = (x - high.astype(jnp.float32)).astype(jnp.bfloat16)
        left = jnp.concatenate([high, low], axis=0)
        total = [jnp.zeros((8, BK), jnp.float32), jnp.zeros((8, BK), jnp.float32)]
        for q in range(8):
            matrix = inv_ref[q // MC, j * MC + q % MC, b]
            product = lax.dot_general(
                left, matrix, (((1,), (1,)), ((), ())), preferred_element_type=jnp.float32
            )
            for d in range(2):
                value = product[d * 8 : d * 8 + 8] + product[16 + d * 8 : 24 + d * 8]
                total[d] = jnp.where(row == q, value, total[d])
        for d in range(2):
            for q in range(8):
                out_ref[q // MC, j * MC + q % MC, d : d + 1, b * BK : (b + 1) * BK] = total[d][q : q + 1]


def mode_order():
    order = []
    for j in range(CHUNKS):
        for h in range(2):
            for f in range(4):
                for s in range(4):
                    x, y = (f, s) if h == 0 else (s, f)
                    order += [((x * 4 + y) * 2 + h) * CHUNKS * MC + j * MC + i for i in range(MC)]
    return np.array(order)


def azimuth_rows():
    table = azimuth_table()[:, :, mode_order()].reshape(NTH, 2, CHUNKS, MTH // CHUNKS)
    return np.ascontiguousarray(table.transpose(2, 1, 3, 0).reshape(CHUNKS, 2 * MTH // CHUNKS, NTH))


def plane_major():
    matrix = np.zeros((BK, 4, 4, BK), np.float32)
    for z in range(4):
        matrix[np.arange(BK), z, z, np.arange(BK)] = 1.0
    return matrix.reshape(4 * BK, 4 * BK).astype(jnp.bfloat16)


def axial_blocks():
    table = axial_table().astype(np.float32)
    blocks = np.zeros((32, KZ, 2, MC, 2, 2, 4, 4, MC), np.float32)
    for device in range(32):
        for source in range(2):
            first = (device ^ source) * 4
            part = table[:, first : first + 4].transpose(2, 3, 0, 1)
            for s in range(4):
                for i in range(MC):
                    blocks[device, :, :, i, source, :, :, s, i] = part
    return blocks.reshape(32, 64, 256)


def whole_kernel(
    forcing_ref, state_hbm, inverses_ref, second_hbm, first_hbm, points_hbm, blocks_ref, rows_ref, order_ref, out_ref,
    state_ref, second_ref, first_ref, points_ref,
    planes_ref, field_ref, table_ref, plane_ref, inv_ref, spectra_ref, weights_ref, explicit_ref, below_ref, above_ref, border_ref, step_ref, block_ref, axial_ref, other_ref, part_ref,
    far_ref, near_ref, line_ref, near2_ref, total_ref, right_ref,
    load_sem, swap_send, swap_recv, send_sem, recv_sem, rad_send, rad_recv,
):
    rad = lax.axis_index("rad")
    mode = lax.axis_index("mode")
    core = mode % 2
    y = (mode // 2) % 4
    x = mode // 8

    def device(xx, yy, cc, zz):
        return (zz, (xx * 4 + yy) * 2 + cc)

    def load(i):
        half = BK // 2
        if i < 4:
            p = (1 - core, core)[i // 2]
            part = pl.ds(i % 2 * half, half)
            src, dst = forcing_ref.at[p, part], planes_ref.at[p, part]
        elif i == 4:
            src, dst = order_ref, plane_ref
        elif i == 5:
            src, dst = blocks_ref.at[mode], block_ref
        else:
            p, part = (i - 6) // 4, pl.ds((i - 6) % 4 * 4, 4)
            src, dst = inverses_ref.at[p, part], inv_ref.at[p, part]
        return pltpu.make_async_copy(src, dst, load_sem.at[i])

    small = ((second_hbm, second_ref), (first_hbm, first_ref), (points_hbm, points_ref), (state_hbm, state_ref))

    def load_small(i):
        return pltpu.make_async_copy(small[i][0], small[i][1], load_sem.at[14 + CHUNKS + i])

    def load_rows(j):
        return pltpu.make_async_copy(rows_ref.at[j], table_ref.at[j], load_sem.at[14 + j])

    load(0).start()
    load(1).start()
    load_rows(0).start()
    load(4).start()
    load(5).start()
    for i in range(4):
        load_small(i).start()

    barrier = pltpu.get_barrier_semaphore()
    sides = [((x + 1) % 4, y), ((x + 3) % 4, y), (x, (y + 1) % 4), (x, (y + 3) % 4)]
    for xx, yy in sides:
        pl.semaphore_signal(barrier, inc=1, device_id=device(xx, yy, core, rad), device_id_type=MESH)
    for dz in range(8):
        for cc in range(2):
            if dz or cc:
                pl.semaphore_signal(
                    barrier, inc=1, device_id=device(x, y, (core + cc) % 2, (rad + dz) % 8), device_id_type=MESH
                )

    def swap(j):
        return pltpu.make_async_remote_copy(
            src_ref=spectra_ref.at[j, 1],
            dst_ref=other_ref.at[j],
            send_sem=swap_send.at[j],
            recv_sem=swap_recv.at[j],
            device_id=device(x, y, 1 - core, rad),
            device_id_type=MESH,
        )

    def merge_planes(p):
        @pl.loop(0, 8)
        def _(i):
            value = planes_ref[p, pl.ds(pl.multiple_of(16 * i, 16), 16)]
            field_ref[p, pl.ds(pl.multiple_of(64 * i, 64), 64)] = value.reshape(64, NTH)

    def azimuth(j, p, which):
        value = lax.dot_general(
            table_ref[j], field_ref[p], (((1,), (1,)), ((), ())), preferred_element_type=jnp.float32
        ).astype(jnp.bfloat16)
        value = jnp.dot(value, plane_ref[...], preferred_element_type=jnp.float32)
        spectra_ref[j, which] = value.astype(jnp.bfloat16)

    load(0).wait()
    load(1).wait()
    load(2).start()
    load(3).start()
    merge_planes(1 - core)
    load(4).wait()
    pl.semaphore_wait(barrier, 19)

    first = (x, y)
    second = (y, x)

    def along(h, leg, step):
        if (h + leg) % 2 == 0:
            return device((x + step) % 4, y, core, rad)
        return device(x, (y + step) % 4, core, rad)

    def copy(j, h, i):
        f = first[h]
        s = second[h]
        leg = i // 6
        step = (1 if i % 2 == 0 else 3) if i < 6 else i - 5
        if i == 0:
            src, dst = part_ref.at[j, h, (f + 2) % 4, pl.ds(0, 2)], far_ref.at[j, h, 0]
        elif i == 1:
            src, dst = part_ref.at[j, h, (f + 2) % 4, pl.ds(2, 2)], far_ref.at[j, h, 1]
        elif i == 2:
            src, dst = part_ref.at[j, h, (f + 1) % 4, pl.ds(2, 2)], near_ref.at[j, h, 0, pl.ds(2, 2)]
        elif i == 3:
            src, dst = part_ref.at[j, h, (f + 3) % 4, pl.ds(0, 2)], near_ref.at[j, h, 1, pl.ds(0, 2)]
        elif i == 4:
            src, dst = part_ref.at[j, h, (f + 1) % 4, pl.ds(0, 2)], near_ref.at[j, h, 0, pl.ds(0, 2)]
        elif i == 5:
            src, dst = part_ref.at[j, h, (f + 3) % 4, pl.ds(2, 2)], near_ref.at[j, h, 1, pl.ds(2, 2)]
        else:
            src, dst = line_ref.at[j, h, (s + i - 5) % 4], near2_ref.at[j, h, i - 6]
        return pltpu.make_async_remote_copy(
            src_ref=src,
            dst_ref=dst,
            send_sem=send_sem.at[j, h, leg],
            recv_sem=recv_sem.at[j, h, i],
            device_id=along(h, leg, step),
            device_id_type=MESH,
        )

    def radial(j, h, dz):
        k = (rad + dz) % 8
        return pltpu.make_async_remote_copy(
            src_ref=total_ref.at[j, h, k],
            dst_ref=right_ref.at[j, rad * 2 + core],
            send_sem=rad_send.at[j, h],
            recv_sem=rad_recv.at[j],
            device_id=device(x, y, h, k),
            device_id_type=MESH,
        )

    def group(j, h, f):
        tiles = []
        for ref in (spectra_ref.at[j, 0], other_ref.at[j]):
            for c in range(2):
                row = pl.ds(pl.multiple_of(c * 128 + h * 64 + f * 16, 16), 16)
                tiles += [ref[row, BK * z : BK * z + BK] for z in range(4)]
        return jnp.concatenate(tiles, axis=0)

    def axial(j):
        swap(j).wait_recv()
        for pair in ((2, 1), (3, 0)):
            for h in range(2):
                f0 = (first[h] + pair[0]) % 4
                f1 = (first[h] + pair[1]) % 4
                right = jnp.concatenate([group(j, h, f0), group(j, h, f1)], axis=1)
                value = jnp.dot(axial_ref[...], right, preferred_element_type=jnp.float32).astype(jnp.bfloat16)
                part_ref[j, h, f0] = value[:, :BK].reshape(4, 64, BK)
                part_ref[j, h, f1] = value[:, BK:].reshape(4, 64, BK)
                for i in (0, 1, 2) if pair[0] == 2 else (3,):
                    copy(j, h, i).start()

    def explicit(j):
        inverse_square = 1.0 / (points_ref[...] * points_ref[...])
        row = lax.broadcasted_iota(jnp.int32, (8, 1), 0)
        index = (mode * CHUNKS * MC + j * MC + row % MC).astype(jnp.float32) * (1.0 / MTH)
        wave = (rad - KZ // 2).astype(jnp.float32)
        shift = index * index * inverse_square + AXIAL_FACTOR * (wave * wave)
        zeros = jnp.zeros((8, BK), jnp.float32)
        for d in range(2):
            state = jnp.concatenate(
                [state_ref[p, j * MC + i, d : d + 1, :] for p in range(2) for i in range(MC)], axis=0
            )
            padded = jnp.concatenate([zeros, state, zeros], axis=1)
            value = state - shift * state
            for o in range(9):
                value = value + weights_ref[o : o + 1, :] * padded[:, BK - 4 + o : BK - 4 + o + NR]
            explicit_ref[j, d] = value

    def add(a, b):
        return (a.astype(jnp.float32) + b.astype(jnp.float32)).astype(jnp.bfloat16)

    def relay(j):
        for h in range(2):
            plus = (first[h] + 1) % 4
            minus = (first[h] + 3) % 4
            copy(j, h, 0).wait_recv()
            part_ref[j, h, plus, 0:2] = add(part_ref[j, h, plus, 0:2], far_ref[j, h, 0])
            copy(j, h, 4).start()
            copy(j, h, 1).wait_recv()
            part_ref[j, h, minus, 2:4] = add(part_ref[j, h, minus, 2:4], far_ref[j, h, 1])
            copy(j, h, 5).start()

    def gather_line(j):
        for h in range(2):
            for i in (2, 3, 4, 5):
                copy(j, h, i).wait_recv()
            value = part_ref[j, h, first[h]].astype(jnp.float32)
            value = value + near_ref[j, h, 0].astype(jnp.float32) + near_ref[j, h, 1].astype(jnp.float32)
            line_ref[j, h] = value.astype(jnp.bfloat16)
            for i in (7, 6, 8):
                copy(j, h, i).start()

    def spread(j):
        for h in range(2):
            for i in (6, 7, 8):
                copy(j, h, i).wait_recv()
            value = line_ref[j, h, second[h]].astype(jnp.float32)
            for i in range(3):
                value = value + near2_ref[j, h, i].astype(jnp.float32)
            total_ref[j, h] = value.astype(jnp.bfloat16).reshape(8, 8, BK)
            for dz in (4, 3, 5, 2, 6, 1, 7):
                radial(j, h, dz).start()

            @pl.when(core == h)
            def _():
                right_ref[j, rad * 2 + core] = total_ref[j, h, rad]

            @pl.when(core != h)
            def _():
                radial(j, h, 0).start()

    def finish(j):
        arrived = right_ref.at[j, pl.ds(0, 15)]
        pltpu.make_async_copy(arrived, arrived, rad_recv.at[j]).wait()
        arrival = [right_ref[j, i].astype(jnp.float32) for i in range(16)]
        rhs = []
        for d in range(2):
            row = slice(4 * d, 4 * d + 4)
            rhs.append(
                [
                    jnp.concatenate([arrival[2 * b][row], arrival[2 * b + 1][row]], axis=0)
                    + explicit_ref[j, d, :, b * BK : (b + 1) * BK]
                    for b in range(NB)
                ]
            )
        solve_chunk(rhs, inv_ref, below_ref, above_ref, border_ref, step_ref, out_ref, j)
        swap(j).wait_send()
        for h in range(2):
            whole = part_ref.at[j, h, pl.ds(0, 3)]
            pltpu.make_async_copy(whole, whole, send_sem.at[j, h, 0]).wait()
            whole = line_ref.at[j, h, pl.ds(0, 3)]
            pltpu.make_async_copy(whole, whole, send_sem.at[j, h, 1]).wait()

            @pl.when(core == h)
            def _():
                whole = total_ref.at[j, h, pl.ds(0, 7)]
                pltpu.make_async_copy(whole, whole, rad_send.at[j, h]).wait()

            @pl.when(core != h)
            def _():
                whole = total_ref.at[j, h]
                pltpu.make_async_copy(whole, whole, rad_send.at[j, h]).wait()

    def send_half(j):
        load_rows(j).wait()
        azimuth(j, 1 - core, 1)
        swap(j).start()

        @pl.when(j < CHUNKS - 1)
        def _():
            load_rows(j + 1).start()

        @pl.when(j == 1)
        def _():
            for i in range(6, 14):
                load(i).start()

    def keep_half(j):
        @pl.when(j == 0)
        def _():
            load(2).wait()
            load(3).wait()
            merge_planes(core)
            load(5).wait()
            place = lax.broadcasted_iota(jnp.int32, (64, 256), 1) // MC % 4
            for s in range(4):
                axial_ref[64 * s : 64 * s + 64] = jnp.where(place == s, block_ref[...], 0.0).astype(jnp.bfloat16)
            for i in range(3):
                load_small(i).wait()
            points = points_ref[...]
            weights = second_ref[...] + first_ref[...] / points
            weights_ref[...] = weights
            below, above = coupling_rows(weights)
            for g in range(4):
                below_ref[g : g + 1, :] = below[g]
                above_ref[g : g + 1, :] = above[g]

        azimuth(j, core, 0)

    def ready(j):
        @pl.when(j == 0)
        def _():
            for i in range(6, 14):
                load(i).wait()
            load_small(3).wait()

        explicit(j)

        @pl.loop(0, NB)
        def _(b):
            prepare(inv_ref, below_ref, above_ref, border_ref, step_ref, j, b)

    stages = [(0, send_half), (1, axial), (0, keep_half), (2, relay), (4, gather_line), (6, spread), (5, ready), (9, finish)]

    @pl.loop(0, CHUNKS + 9)
    def _(tick):
        for delay, stage in stages:
            j = tick - delay

            @pl.when((j >= 0) & (j < CHUNKS))
            def _():
                stage(j)


def transform_and_solve(forcing, state, inverses, second_weights, first_weights, points, blocks, rows, order):
    bf16 = jnp.bfloat16
    tile = (CHUNKS, 2)
    vmem = pl.BlockSpec(memory_space=pltpu.VMEM)
    anywhere = pl.BlockSpec(memory_space=pl.ANY)
    return pl.pallas_call(
        whole_kernel,
        out_shape=jax.ShapeDtypeStruct(state.shape, jnp.float32),
        in_specs=[anywhere] * 9,
        out_specs=vmem,
        scratch_shapes=[
            pltpu.VMEM(state.shape, jnp.float32),
            pltpu.VMEM((9, NR), jnp.float32),
            pltpu.VMEM((9, NR), jnp.float32),
            pltpu.VMEM((1, NR), jnp.float32),
            pltpu.VMEM(forcing.shape, bf16),
            pltpu.VMEM((2, 4 * BK, NTH), bf16),
            pltpu.VMEM(rows.shape, bf16),
            pltpu.VMEM(order.shape, bf16),
            pltpu.VMEM(inverses.shape, bf16),
            pltpu.VMEM((CHUNKS, 2, 256, 4 * BK), bf16),
            pltpu.VMEM((9, NR), jnp.float32),
            pltpu.VMEM((CHUNKS, 2, 8, NR), jnp.float32),
            pltpu.VMEM((8, NR), jnp.float32),
            pltpu.VMEM((8, NR), jnp.float32),
            pltpu.VMEM((CHUNKS, NB, 8, 8, BK), jnp.float32),
            pltpu.VMEM((CHUNKS, NB, 3, 4, 4, 8, BK), jnp.float32),
            pltpu.VMEM((64, 256), jnp.float32),
            pltpu.VMEM((256, 256), bf16),
            pltpu.VMEM((CHUNKS, 256, 4 * BK), bf16),
            pltpu.VMEM(tile + (4, 4, 64, BK), bf16),
            pltpu.VMEM(tile + (2, 2, 64, BK), bf16),
            pltpu.VMEM(tile + (2, 4, 64, BK), bf16),
            pltpu.VMEM(tile + (4, 64, BK), bf16),
            pltpu.VMEM(tile + (3, 64, BK), bf16),
            pltpu.VMEM(tile + (8, 8, BK), bf16),
            pltpu.VMEM((CHUNKS, 16, 8, BK), bf16),
            pltpu.SemaphoreType.DMA((18 + CHUNKS,)),
            pltpu.SemaphoreType.DMA((CHUNKS,)),
            pltpu.SemaphoreType.DMA((CHUNKS,)),
            pltpu.SemaphoreType.DMA((CHUNKS, 2, 2)),
            pltpu.SemaphoreType.DMA((CHUNKS, 2, 9)),
            pltpu.SemaphoreType.DMA((CHUNKS, 2)),
            pltpu.SemaphoreType.DMA((CHUNKS,)),
        ],
        compiler_params=pltpu.CompilerParams(
            vmem_limit_bytes=60 * 2**20, collective_id=0, has_side_effects=True
        ),
        name="transform_and_solve",
    )(forcing, state, inverses, second_weights, first_weights, points, blocks, rows, order)


def body(forcing, spectral_state, block_inverses, second_weights, first_weights, radial_points):
    mode_count = MTH // lax.axis_size("mode")
    out = transform_and_solve(
        forcing,
        spectral_state.reshape(2, mode_count, 2, NR),
        block_inverses.reshape(2, mode_count, NB, BK, BK),
        second_weights,
        first_weights,
        radial_points.reshape(1, NR),
        jnp.asarray(axial_blocks()),
        jnp.asarray(azimuth_rows()),
        jnp.asarray(plane_major()),
    )
    return out.reshape(2, mode_count, 1, 2, NR)


def solution(mesh):
    return jax.shard_map(
        body,
        mesh=mesh,
        in_specs=(
            P(None, "rad", "mode", None),
            P(None, "mode", "rad", None, None),
            P(None, "mode", "rad", None, None, None),
            P(),
            P(),
            P(),
        ),
        out_specs=P(None, "mode", "rad", None, None),
        check_vma=False,
    )
```

```python
import math

import jax
import jax.numpy as jnp
import numpy as np
from jax import lax
from jax.experimental import pallas as pl
from jax.experimental.pallas import tpu as pltpu
from jax.sharding import PartitionSpec as P

NTH = 1536
MTH = 512
NZ = 128
KZ = 8
BK = 128
NB = 8
NR = 1024
CHUNKS = 4
MC = 4


AXIAL_FACTOR = 0.05
MESH = pl.DeviceIdType.MESH


def azimuth_table():
    t = np.arange(NTH, dtype=np.int64)[:, None]
    m = np.arange(MTH, dtype=np.int64)[None, :]
    radians = 2.0 * math.pi / NTH * ((t * m) % NTH).astype(np.float64)
    norm = 1.0 / math.sqrt(NTH)
    table = np.stack([np.cos(radians) * norm, -np.sin(radians) * norm], axis=1)
    return table.astype(np.float32).astype(jnp.bfloat16)


def axial_table():
    z = np.arange(NZ, dtype=np.int64)[:, None]
    q = np.arange(KZ, dtype=np.int64)[None, :] - KZ // 2
    radians = 2.0 * math.pi / NZ * (((q % NZ) * z) % NZ).astype(np.float64)
    norm = 1.0 / math.sqrt(NZ)
    c = np.cos(radians) * norm
    s = np.sin(radians) * norm
    table = np.stack([np.stack([c, -s], axis=-1), np.stack([s, c], axis=-1)], axis=0)
    return table.astype(np.float32).astype(jnp.bfloat16)


def border_rows(inv_ref, j, b):
    per_problem = []
    for p in range(2):
        for i in range(MC):
            top = inv_ref[p, j * MC + i, b, 0:16, :].astype(jnp.float32)
            low = inv_ref[p, j * MC + i, b, BK - 16 : BK, :].astype(jnp.float32)
            per_problem.append(jnp.concatenate([top[0:4], low[12:16]], axis=0))
    return jnp.swapaxes(jnp.stack(per_problem, axis=0), 0, 1)


def coupling_rows(weights):
    place = lax.broadcasted_iota(jnp.int32, (1, NR), 1) % BK
    below, above = [], []
    for g in range(4):
        m = jnp.zeros((1, NR), jnp.float32)
        n = jnp.zeros((1, NR), jnp.float32)
        for a in range(4):
            if g >= a:
                m = jnp.where(place == a, -weights[g - a : g - a + 1, :], m)
            if g <= a:
                n = jnp.where(place == BK - 4 + a, -weights[g - a + 8 : g - a + 9, :], n)
        below.append(m)
        above.append(n)
    return below, above


def lane_sum(value):
    return jnp.sum(value, axis=-1, keepdims=True)


def prepare(inv_ref, below_ref, above_ref, border_ref, step_ref, j, b):
    rows = border_rows(inv_ref, j, b)
    border_ref[j, b] = rows
    lanes = pl.ds(pl.multiple_of(b * BK, BK), BK)
    for g in range(4):
        m = below_ref[g : g + 1, lanes]
        n = above_ref[g : g + 1, lanes]
        for a in range(4):
            shape = (8, BK)
            step_ref[j, b, 0, a, g] = jnp.broadcast_to(lane_sum(rows[4 + a] * m), shape)
            step_ref[j, b, 1, a, g] = jnp.broadcast_to(lane_sum(rows[a] * m), shape)
            step_ref[j, b, 2, a, g] = jnp.broadcast_to(lane_sum(rows[a] * n), shape)


def solve_chunk(rhs, inv_ref, below_ref, above_ref, border_ref, step_ref, out_ref, j):
    shape = (8, BK)
    corrected = [[None] * NB for _ in range(2)]
    for d in range(2):
        tails = []
        heads = []
        for b in range(NB):
            x = rhs[d][b]
            tail = None
            if b < NB - 1:
                tail = [jnp.broadcast_to(lane_sum(border_ref[j, b, 4 + a] * x), shape) for a in range(4)]
            head = [jnp.broadcast_to(lane_sum(border_ref[j, b, a] * x), shape) for a in range(4)]
            tails.append(tail)
            heads.append(head)
        for b in range(1, NB):
            prev = tails[b - 1]
            if b < NB - 1:
                tails[b] = [
                    tails[b][a] - sum(step_ref[j, b, 0, a, g] * prev[g] for g in range(4)) for a in range(4)
                ]
            heads[b] = [heads[b][a] - sum(step_ref[j, b, 1, a, g] * prev[g] for g in range(4)) for a in range(4)]
        for b in range(NB - 2, 0, -1):
            nxt = heads[b + 1]
            heads[b] = [heads[b][a] - sum(step_ref[j, b, 2, a, g] * nxt[g] for g in range(4)) for a in range(4)]
        for b in range(NB):
            x = rhs[d][b]
            lanes = slice(b * BK, (b + 1) * BK)
            if b > 0:
                x = x - sum(tails[b - 1][g] * below_ref[g : g + 1, lanes] for g in range(4))
            if b < NB - 1:
                x = x - sum(heads[b + 1][g] * above_ref[g : g + 1, lanes] for g in range(4))
            corrected[d][b] = x
    row = lax.broadcasted_iota(jnp.int32, (8, BK), 0)
    for b in range(NB):
        x = jnp.concatenate([corrected[0][b], corrected[1][b]], axis=0)
        high = x.astype(jnp.bfloat16)
        low = (x - high.astype(jnp.float32)).astype(jnp.bfloat16)
        left = jnp.concatenate([high, low], axis=0)
        total = [jnp.zeros((8, BK), jnp.float32), jnp.zeros((8, BK), jnp.float32)]
        for q in range(8):
            matrix = inv_ref[q // MC, j * MC + q % MC, b]
            product = lax.dot_general(
                left, matrix, (((1,), (1,)), ((), ())), preferred_element_type=jnp.float32
            )
            for d in range(2):
                value = product[d * 8 : d * 8 + 8] + product[16 + d * 8 : 24 + d * 8]
                total[d] = jnp.where(row == q, value, total[d])
        for d in range(2):
            for q in range(8):
                out_ref[q // MC, j * MC + q % MC, d : d + 1, b * BK : (b + 1) * BK] = total[d][q : q + 1]


def mode_order():
    order = []
    for j in range(CHUNKS):
        for h in range(2):
            for f in range(4):
                for s in range(4):
                    x, y = (f, s) if h == 0 else (s, f)
                    order += [((x * 4 + y) * 2 + h) * CHUNKS * MC + j * MC + i for i in range(MC)]
    return np.array(order)


def azimuth_rows():
    table = azimuth_table()[:, :, mode_order()].reshape(NTH, 2, CHUNKS, MTH // CHUNKS)
    return np.ascontiguousarray(table.transpose(2, 1, 3, 0).reshape(CHUNKS, 2 * MTH // CHUNKS, NTH))


def plane_major():
    matrix = np.zeros((BK, 4, 4, BK), np.float32)
    for z in range(4):
        matrix[np.arange(BK), z, z, np.arange(BK)] = 1.0
    return matrix.reshape(4 * BK, 4 * BK).astype(jnp.bfloat16)


def axial_blocks():
    table = axial_table().astype(np.float32)
    blocks = np.zeros((32, KZ, 2, MC, 2, 2, 4, 4, MC), np.float32)
    for device in range(32):
        for source in range(2):
            first = (device ^ source) * 4
            part = table[:, first : first + 4].transpose(2, 3, 0, 1)
            for s in range(4):
                for i in range(MC):
                    blocks[device, :, :, i, source, :, :, s, i] = part
    return blocks.reshape(32, 64, 256)


def whole_kernel(
    forcing_ref, state_hbm, inverses_ref, second_hbm, first_hbm, points_hbm, blocks_ref, rows_ref, order_ref, out_ref,
    state_ref, second_ref, first_ref, points_ref,
    planes_ref, field_ref, table_ref, plane_ref, inv_ref, spectra_ref, weights_ref, explicit_ref, below_ref, above_ref, border_ref, step_ref, block_ref, axial_ref, other_ref, part_ref,
    far_ref, near_ref, line_ref, near2_ref, total_ref, right_ref,
    load_sem, swap_send, swap_recv, send_sem, recv_sem, rad_send, rad_recv,
):
    rad = lax.axis_index("rad")
    mode = lax.axis_index("mode")
    core = mode % 2
    y = (mode // 2) % 4
    x = mode // 8

    def device(xx, yy, cc, zz):
        return (zz, (xx * 4 + yy) * 2 + cc)

    def load(i):
        half = BK // 2
        if i < 4:
            p = (1 - core, core)[i // 2]
            part = pl.ds(i % 2 * half, half)
            src, dst = forcing_ref.at[p, part], planes_ref.at[p, part]
        elif i == 4:
            src, dst = order_ref, plane_ref
        elif i == 5:
            src, dst = blocks_ref.at[mode], block_ref
        else:
            p, part = (i - 6) // 4, pl.ds((i - 6) % 4 * 4, 4)
            src, dst = inverses_ref.at[p, part], inv_ref.at[p, part]
        return pltpu.make_async_copy(src, dst, load_sem.at[i])

    small = ((second_hbm, second_ref), (first_hbm, first_ref), (points_hbm, points_ref), (state_hbm, state_ref))

    def load_small(i):
        return pltpu.make_async_copy(small[i][0], small[i][1], load_sem.at[14 + CHUNKS + i])

    def load_rows(j):
        return pltpu.make_async_copy(rows_ref.at[j], table_ref.at[j], load_sem.at[14 + j])

    load(0).start()
    load(1).start()
    load_rows(0).start()
    load(4).start()
    load(5).start()
    for i in range(4):
        load_small(i).start()

    barrier = pltpu.get_barrier_semaphore()
    sides = [((x + 1) % 4, y), ((x + 3) % 4, y), (x, (y + 1) % 4), (x, (y + 3) % 4)]
    for xx, yy in sides:
        pl.semaphore_signal(barrier, inc=1, device_id=device(xx, yy, core, rad), device_id_type=MESH)
    for dz in range(8):
        for cc in range(2):
            if dz or cc:
                pl.semaphore_signal(
                    barrier, inc=1, device_id=device(x, y, (core + cc) % 2, (rad + dz) % 8), device_id_type=MESH
                )

    def swap(j):
        return pltpu.make_async_remote_copy(
            src_ref=spectra_ref.at[j, 1],
            dst_ref=other_ref.at[j],
            send_sem=swap_send.at[j],
            recv_sem=swap_recv.at[j],
            device_id=device(x, y, 1 - core, rad),
            device_id_type=MESH,
        )

    def merge_planes(p, half):
        @pl.loop(4 * half, 4 * half + 4)
        def _(i):
            value = planes_ref[p, pl.ds(pl.multiple_of(16 * i, 16), 16)]
            field_ref[p, pl.ds(pl.multiple_of(64 * i, 64), 64)] = value.reshape(64, NTH)

    def azimuth(j, p, which):
        value = lax.dot_general(
            table_ref[j], field_ref[p], (((1,), (1,)), ((), ())), preferred_element_type=jnp.float32
        ).astype(jnp.bfloat16)
        value = jnp.dot(value, plane_ref[...], preferred_element_type=jnp.float32)
        spectra_ref[j, which] = value.astype(jnp.bfloat16)

    load(0).wait()
    merge_planes(1 - core, 0)
    load(1).wait()
    load(2).start()
    load(3).start()
    merge_planes(1 - core, 1)
    load(4).wait()
    pl.semaphore_wait(barrier, 19)

    first = (x, y)
    second = (y, x)

    def along(h, leg, step):
        if (h + leg) % 2 == 0:
            return device((x + step) % 4, y, core, rad)
        return device(x, (y + step) % 4, core, rad)

    def copy(j, h, i):
        f = first[h]
        s = second[h]
        leg = i // 6
        step = (1 if i % 2 == 0 else 3) if i < 6 else i - 5
        if i == 0:
            src, dst = part_ref.at[j, h, (f + 2) % 4, pl.ds(0, 2)], far_ref.at[j, h, 0]
        elif i == 1:
            src, dst = part_ref.at[j, h, (f + 2) % 4, pl.ds(2, 2)], far_ref.at[j, h, 1]
        elif i == 2:
            src, dst = part_ref.at[j, h, (f + 1) % 4, pl.ds(2, 2)], near_ref.at[j, h, 0, pl.ds(2, 2)]
        elif i == 3:
            src, dst = part_ref.at[j, h, (f + 3) % 4, pl.ds(0, 2)], near_ref.at[j, h, 1, pl.ds(0, 2)]
        elif i == 4:
            src, dst = part_ref.at[j, h, (f + 1) % 4, pl.ds(0, 2)], near_ref.at[j, h, 0, pl.ds(0, 2)]
        elif i == 5:
            src, dst = part_ref.at[j, h, (f + 3) % 4, pl.ds(2, 2)], near_ref.at[j, h, 1, pl.ds(2, 2)]
        else:
            src, dst = line_ref.at[j, h, (s + i - 5) % 4], near2_ref.at[j, h, i - 6]
        return pltpu.make_async_remote_copy(
            src_ref=src,
            dst_ref=dst,
            send_sem=send_sem.at[j, h, leg],
            recv_sem=recv_sem.at[j, h, i],
            device_id=along(h, leg, step),
            device_id_type=MESH,
        )

    def radial(j, h, dz):
        k = (rad + dz) % 8
        return pltpu.make_async_remote_copy(
            src_ref=total_ref.at[j, h, k],
            dst_ref=right_ref.at[j, rad * 2 + core],
            send_sem=rad_send.at[j, h],
            recv_sem=rad_recv.at[j],
            device_id=device(x, y, h, k),
            device_id_type=MESH,
        )

    def group(j, h, f):
        tiles = []
        for ref in (spectra_ref.at[j, 0], other_ref.at[j]):
            for c in range(2):
                row = pl.ds(pl.multiple_of(c * 128 + h * 64 + f * 16, 16), 16)
                tiles += [ref[row, BK * z : BK * z + BK] for z in range(4)]
        return jnp.concatenate(tiles, axis=0)

    def axial(j):
        swap(j).wait_recv()
        for pair in ((2, 1), (3, 0)):
            for h in range(2):
                f0 = (first[h] + pair[0]) % 4
                f1 = (first[h] + pair[1]) % 4
                right = jnp.concatenate([group(j, h, f0), group(j, h, f1)], axis=1)
                value = jnp.dot(axial_ref[...], right, preferred_element_type=jnp.float32).astype(jnp.bfloat16)
                part_ref[j, h, f0] = value[:, :BK].reshape(4, 64, BK)
                part_ref[j, h, f1] = value[:, BK:].reshape(4, 64, BK)
                for i in (0, 1, 2) if pair[0] == 2 else (3,):
                    copy(j, h, i).start()

    def explicit(j):
        inverse_square = 1.0 / (points_ref[...] * points_ref[...])
        row = lax.broadcasted_iota(jnp.int32, (8, 1), 0)
        index = (mode * CHUNKS * MC + j * MC + row % MC).astype(jnp.float32) * (1.0 / MTH)
        wave = (rad - KZ // 2).astype(jnp.float32)
        shift = index * index * inverse_square + AXIAL_FACTOR * (wave * wave)
        zeros = jnp.zeros((8, BK), jnp.float32)
        for d in range(2):
            state = jnp.concatenate(
                [state_ref[p, j * MC + i, d : d + 1, :] for p in range(2) for i in range(MC)], axis=0
            )
            padded = jnp.concatenate([zeros, state, zeros], axis=1)
            value = state - shift * state
            for o in range(9):
                value = value + weights_ref[o : o + 1, :] * padded[:, BK - 4 + o : BK - 4 + o + NR]
            explicit_ref[j, d] = value

    def add(a, b):
        return (a.astype(jnp.float32) + b.astype(jnp.float32)).astype(jnp.bfloat16)

    def relay(j):
        for h in range(2):
            plus = (first[h] + 1) % 4
            minus = (first[h] + 3) % 4
            copy(j, h, 0).wait_recv()
            part_ref[j, h, plus, 0:2] = add(part_ref[j, h, plus, 0:2], far_ref[j, h, 0])
            copy(j, h, 4).start()
            copy(j, h, 1).wait_recv()
            part_ref[j, h, minus, 2:4] = add(part_ref[j, h, minus, 2:4], far_ref[j, h, 1])
            copy(j, h, 5).start()

    def gather_line(j):
        for h in range(2):
            for i in (2, 3, 4, 5):
                copy(j, h, i).wait_recv()
            value = part_ref[j, h, first[h]].astype(jnp.float32)
            value = value + near_ref[j, h, 0].astype(jnp.float32) + near_ref[j, h, 1].astype(jnp.float32)
            line_ref[j, h] = value.astype(jnp.bfloat16)
            for i in (7, 6, 8):
                copy(j, h, i).start()

    def spread(j):
        for h in range(2):
            for i in (6, 7, 8):
                copy(j, h, i).wait_recv()
            value = line_ref[j, h, second[h]].astype(jnp.float32)
            for i in range(3):
                value = value + near2_ref[j, h, i].astype(jnp.float32)
            total_ref[j, h] = value.astype(jnp.bfloat16).reshape(8, 8, BK)
            for dz in (4, 3, 5, 2, 6, 1, 7):
                radial(j, h, dz).start()

            @pl.when(core == h)
            def _():
                right_ref[j, rad * 2 + core] = total_ref[j, h, rad]

            @pl.when(core != h)
            def _():
                radial(j, h, 0).start()

    def finish(j):
        arrived = right_ref.at[j, pl.ds(0, 15)]
        pltpu.make_async_copy(arrived, arrived, rad_recv.at[j]).wait()
        arrival = [right_ref[j, i].astype(jnp.float32) for i in range(16)]
        rhs = []
        for d in range(2):
            row = slice(4 * d, 4 * d + 4)
            rhs.append(
                [
                    jnp.concatenate([arrival[2 * b][row], arrival[2 * b + 1][row]], axis=0)
                    + explicit_ref[j, d, :, b * BK : (b + 1) * BK]
                    for b in range(NB)
                ]
            )
        solve_chunk(rhs, inv_ref, below_ref, above_ref, border_ref, step_ref, out_ref, j)
        swap(j).wait_send()
        for h in range(2):
            whole = part_ref.at[j, h, pl.ds(0, 3)]
            pltpu.make_async_copy(whole, whole, send_sem.at[j, h, 0]).wait()
            whole = line_ref.at[j, h, pl.ds(0, 3)]
            pltpu.make_async_copy(whole, whole, send_sem.at[j, h, 1]).wait()

            @pl.when(core == h)
            def _():
                whole = total_ref.at[j, h, pl.ds(0, 7)]
                pltpu.make_async_copy(whole, whole, rad_send.at[j, h]).wait()

            @pl.when(core != h)
            def _():
                whole = total_ref.at[j, h]
                pltpu.make_async_copy(whole, whole, rad_send.at[j, h]).wait()

    def send_half(j):
        load_rows(j).wait()
        azimuth(j, 1 - core, 1)
        swap(j).start()

        @pl.when(j < CHUNKS - 1)
        def _():
            load_rows(j + 1).start()

        @pl.when(j == 1)
        def _():
            for i in range(6, 14):
                load(i).start()

    def keep_half(j):
        @pl.when(j == 0)
        def _():
            load(2).wait()
            merge_planes(core, 0)
            load(3).wait()
            merge_planes(core, 1)
            load(5).wait()
            place = lax.broadcasted_iota(jnp.int32, (64, 256), 1) // MC % 4
            for s in range(4):
                axial_ref[64 * s : 64 * s + 64] = jnp.where(place == s, block_ref[...], 0.0).astype(jnp.bfloat16)
            for i in range(3):
                load_small(i).wait()
            points = points_ref[...]
            weights = second_ref[...] + first_ref[...] / points
            weights_ref[...] = weights
            below, above = coupling_rows(weights)
            for g in range(4):
                below_ref[g : g + 1, :] = below[g]
                above_ref[g : g + 1, :] = above[g]

        azimuth(j, core, 0)

    def ready(j):
        @pl.when(j == 0)
        def _():
            for i in range(6, 14):
                load(i).wait()
            load_small(3).wait()

        explicit(j)

        @pl.loop(0, NB)
        def _(b):
            prepare(inv_ref, below_ref, above_ref, border_ref, step_ref, j, b)

    stages = [(0, send_half), (1, axial), (0, keep_half), (2, relay), (4, gather_line), (6, spread), (6, ready), (9, finish)]

    @pl.loop(0, CHUNKS + 9)
    def _(tick):
        for delay, stage in stages:
            j = tick - delay

            @pl.when((j >= 0) & (j < CHUNKS))
            def _():
                stage(j)


def transform_and_solve(forcing, state, inverses, second_weights, first_weights, points, blocks, rows, order):
    bf16 = jnp.bfloat16
    tile = (CHUNKS, 2)
    vmem = pl.BlockSpec(memory_space=pltpu.VMEM)
    anywhere = pl.BlockSpec(memory_space=pl.ANY)
    return pl.pallas_call(
        whole_kernel,
        out_shape=jax.ShapeDtypeStruct(state.shape, jnp.float32),
        in_specs=[anywhere] * 9,
        out_specs=vmem,
        scratch_shapes=[
            pltpu.VMEM(state.shape, jnp.float32),
            pltpu.VMEM((9, NR), jnp.float32),
            pltpu.VMEM((9, NR), jnp.float32),
            pltpu.VMEM((1, NR), jnp.float32),
            pltpu.VMEM(forcing.shape, bf16),
            pltpu.VMEM((2, 4 * BK, NTH), bf16),
            pltpu.VMEM(rows.shape, bf16),
            pltpu.VMEM(order.shape, bf16),
            pltpu.VMEM(inverses.shape, bf16),
            pltpu.VMEM((CHUNKS, 2, 256, 4 * BK), bf16),
            pltpu.VMEM((9, NR), jnp.float32),
            pltpu.VMEM((CHUNKS, 2, 8, NR), jnp.float32),
            pltpu.VMEM((8, NR), jnp.float32),
            pltpu.VMEM((8, NR), jnp.float32),
            pltpu.VMEM((CHUNKS, NB, 8, 8, BK), jnp.float32),
            pltpu.VMEM((CHUNKS, NB, 3, 4, 4, 8, BK), jnp.float32),
            pltpu.VMEM((64, 256), jnp.float32),
            pltpu.VMEM((256, 256), bf16),
            pltpu.VMEM((CHUNKS, 256, 4 * BK), bf16),
            pltpu.VMEM(tile + (4, 4, 64, BK), bf16),
            pltpu.VMEM(tile + (2, 2, 64, BK), bf16),
            pltpu.VMEM(tile + (2, 4, 64, BK), bf16),
            pltpu.VMEM(tile + (4, 64, BK), bf16),
            pltpu.VMEM(tile + (3, 64, BK), bf16),
            pltpu.VMEM(tile + (8, 8, BK), bf16),
            pltpu.VMEM((CHUNKS, 16, 8, BK), bf16),
            pltpu.SemaphoreType.DMA((18 + CHUNKS,)),
            pltpu.SemaphoreType.DMA((CHUNKS,)),
            pltpu.SemaphoreType.DMA((CHUNKS,)),
            pltpu.SemaphoreType.DMA((CHUNKS, 2, 2)),
            pltpu.SemaphoreType.DMA((CHUNKS, 2, 9)),
            pltpu.SemaphoreType.DMA((CHUNKS, 2)),
            pltpu.SemaphoreType.DMA((CHUNKS,)),
        ],
        compiler_params=pltpu.CompilerParams(
            vmem_limit_bytes=60 * 2**20, collective_id=0, has_side_effects=True
        ),
        name="transform_and_solve",
    )(forcing, state, inverses, second_weights, first_weights, points, blocks, rows, order)


def body(forcing, spectral_state, block_inverses, second_weights, first_weights, radial_points):
    mode_count = MTH // lax.axis_size("mode")
    out = transform_and_solve(
        forcing,
        spectral_state.reshape(2, mode_count, 2, NR),
        block_inverses.reshape(2, mode_count, NB, BK, BK),
        second_weights,
        first_weights,
        radial_points.reshape(1, NR),
        jnp.asarray(axial_blocks()),
        jnp.asarray(azimuth_rows()),
        jnp.asarray(plane_major()),
    )
    return out.reshape(2, mode_count, 1, 2, NR)


def solution(mesh):
    return jax.shard_map(
        body,
        mesh=mesh,
        in_specs=(
            P(None, "rad", "mode", None),
            P(None, "mode", "rad", None, None),
            P(None, "mode", "rad", None, None, None),
            P(),
            P(),
            P(),
        ),
        out_specs=P(None, "mode", "rad", None, None),
        check_vma=False,
    )
```
